1024 devices in a mesh: group: 8 (over x, core), inner: 128 (over z, y).
Axes of the slice: x: 4, y: 4, z: 32, core: 2. Of those that a mesh axis runs over, the one named last changes fastest.
Arguments:
- out_grad: bfloat16 [2048, 3584], P(('group', 'inner')), may hold values from -6 to 6
- routing_weight: bfloat16 [2048, 8], P(('group', 'inner')), may hold values from 0.099609375 to 1
- expert_ids: int32 [2048, 8], P(('group', 'inner')), may hold values from 0 to 127, as said below
- slot_index: int32 [2048, 8], P(('group', 'inner')), may hold values from 0 to 23, as said below
- w_gate: bfloat16 [3584, 131072], P(None, ('group', 'inner')), may hold values from -0.09375 to 0.09375
- w_up: bfloat16 [3584, 131072], P(None, ('group', 'inner')), may hold values from -0.09375 to 0.09375
- w_down: bfloat16 [131072, 3584], P(('group', 'inner')), may hold values from -0.1875 to 0.1875
- pre_act: bfloat16 [2, 192, 131072], P(None, None, ('group', 'inner')), may hold values from -5 to 5
Outputs:
- grad_tokens: bfloat16 [2048, 3584], P(('group', 'inner'))
- grad_routing: float32 [2048, 8], P(('group', 'inner'))
The draws below stay inside these ranges and needn't reach their ends.
Inputs may be any that keep to these rules, and one draw needn't show every extreme that they name: `expert_ids`: each token names 8 different experts, two in each of 4 different node groups (expert e lies in group e // 16). Among the 256 tokens of one index of group, every node group is named by exactly half of the tokens, and in every node group half of the experts are named by exactly 24 of these tokens and the other half by 8. slot_index[t, k] is the number of tokens before t, among the 256 tokens of the same index of group, that name expert expert_ids[t, k].
All inputs are finite; a program needn't handle non-finite values.
Results may differ from the reference program's by a relative error of at most 0.0075.
Values may be sent and summed in bfloat16 or wider, within the bound.
A program may use at most 32 MiB of HBM per device.

```python
import math
import jax
import jax.numpy as jnp
from jax import lax

D = 3584
HID_DEV = 128
SPLIT = 8
FF = 1024
EXP_GROUP = 16
EXPERTS = 128
TOPG = 4
TOPK = 8
BLOCK = 256
CAP = 24
TOKENS = 2048
N_GROUP = 8


def block_route(key):
    key_pos, key_group, key_order = jax.random.split(key, 3)
    position = jax.random.permutation(key_pos, BLOCK).astype(jnp.int32)
    relabel = jax.random.permutation(key_group, N_GROUP).astype(jnp.int32)
    offsets = jnp.arange(TOPG, dtype=jnp.int32)
    chosen = relabel[(position[:, None] + offsets[None, :]) % N_GROUP]
    member = jnp.any(chosen[:, :, None] == jnp.arange(N_GROUP, dtype=jnp.int32)[None, None, :], axis=1).astype(jnp.int32)
    ranking = jnp.cumsum(member, axis=0) - member
    order_keys = jax.random.split(key_order, N_GROUP)
    orders = jax.vmap(lambda one_key: jax.random.permutation(one_key, EXP_GROUP).astype(jnp.int32))(order_keys)
    loads = jnp.where(jnp.arange(EXP_GROUP) < EXP_GROUP // 2, CAP, CAP // 3).astype(jnp.int32)
    listing = jax.vmap(lambda order_row: jnp.repeat(order_row, loads, total_repeat_length=BLOCK))(orders)
    rank_sel = jnp.take_along_axis(ranking, chosen, axis=1)
    first_pick = listing[chosen, rank_sel]
    second_pick = listing[chosen, rank_sel + BLOCK // 2]
    local_ids = jnp.stack([first_pick, second_pick], axis=-1).reshape(BLOCK, TOPK)
    group_ids = jnp.repeat(chosen, 2, axis=1)
    expert_table = (group_ids * EXP_GROUP + local_ids).astype(jnp.int32)
    hits = jnp.any(expert_table[:, :, None] == jnp.arange(EXPERTS, dtype=jnp.int32)[None, None, :], axis=1).astype(jnp.int32)
    before = jnp.cumsum(hits, axis=0) - hits
    slot_table = jnp.take_along_axis(before, expert_table, axis=1).astype(jnp.int32)
    return (expert_table, slot_table)


def routing_tables(key):
    block_keys = jax.random.split(key, N_GROUP)
    expert_table, slot_table = jax.vmap(block_route)(block_keys)
    return (expert_table.reshape(TOKENS, TOPK), slot_table.reshape(TOKENS, TOPK))


def draw_expert_ids(key, part):
    shared = routing_tables(key)
    return shared[0]


def draw_slot_index(key, part):
    shared = routing_tables(key)
    return shared[1]


def levels(rng, dims, cuts, smallest, high):
    gain, own = 1.0, jax.random.fold_in(rng, 6)
    for axis_at, parts in cuts:
        draws = jnp.exp(jax.random.uniform(jax.random.fold_in(own, axis_at), (parts,), jnp.float32, smallest / len(cuts), high / len(cuts)))
        gain = gain * jnp.repeat(draws, dims[axis_at] // parts).reshape([-1 if axis == axis_at else 1 for axis in range(len(dims))])
    return gain


def scatter_about(key, dims, spread, limit, cuts=(), kind=jnp.bfloat16):
    array = jax.random.normal(key, dims, jnp.float32) * spread
    if len(cuts) > 0:
        array = levels(key, dims, cuts, -0.22, 0.18) * array
    return jnp.clip(array, min=-limit, max=limit).astype(kind)


def setup_inputs(seed: int = 0) -> dict:
    streams_of = jax.random.split(jax.random.key(seed), 9)
    out_grad = scatter_about(streams_of[0], (TOKENS, D), 1.0, 6.0, ((0, 1024),))
    routing_weight = jnp.clip(jnp.exp(math.log(1.0) - 2.306499 * jax.random.uniform(streams_of[1], (TOKENS, TOPK), jnp.float32) ** levels(streams_of[1], (TOKENS, TOPK), ((0, 1024),), -0.2, 0.2)), 0.099609375, 1.0).astype(jnp.bfloat16)
    expert_ids = draw_expert_ids(jax.random.fold_in(streams_of[8], 71), 0)
    slot_index = draw_slot_index(jax.random.fold_in(streams_of[8], 71), 0)
    w_gate = scatter_about(streams_of[4], (D, EXPERTS * FF), D ** -0.5, 0.09375, ((1, 1024),))
    w_up = scatter_about(streams_of[5], (D, EXPERTS * FF), D ** -0.5, 0.09375, ((1, 1024),))
    w_down = scatter_about(streams_of[6], (EXPERTS * FF, D), FF ** -0.5, 0.1875, ((0, 1024),))
    pre_act = scatter_about(streams_of[7], (2, N_GROUP * CAP, EXPERTS * FF), 1.0, 5.0, ((2, 1024),))
    return dict(out_grad=out_grad, routing_weight=routing_weight, expert_ids=expert_ids, slot_index=slot_index, w_gate=w_gate, w_up=w_up, w_down=w_down, pre_act=pre_act)


def expert_backward(token_rows, weight, gate_weight, up_weight, down_weight, saved_pre):
    highest = lax.Precision.HIGHEST
    slot_rows = token_rows.shape[0]
    back_proj = jnp.dot(token_rows, down_weight.T, preferred_element_type=jnp.float32)
    pre_gate = saved_pre[0].astype(jnp.float32)
    pre_up = saved_pre[1].astype(jnp.float32)
    gate_sig = jax.nn.sigmoid(pre_gate)
    swish_gate = pre_gate * gate_sig
    hidden = swish_gate * pre_up
    gate_blocks = jnp.sum((hidden * back_proj).reshape(slot_rows, SPLIT, HID_DEV), axis=2).astype(jnp.bfloat16)
    gate_blocks = lax.optimization_barrier(gate_blocks)
    gate_term = jnp.sum(gate_blocks.astype(jnp.float32), axis=1)
    scaled = weight[:, None] * back_proj
    grad_up = (scaled * swish_gate).astype(jnp.bfloat16)
    grad_gate = (scaled * pre_up * gate_sig * (1.0 + pre_gate * (1.0 - gate_sig))).astype(jnp.bfloat16)
    gate_split = grad_gate.astype(jnp.float32).reshape(slot_rows, SPLIT, HID_DEV)
    up_split = grad_up.astype(jnp.float32).reshape(slot_rows, SPLIT, HID_DEV)
    gate_w_split = gate_weight.astype(jnp.float32).reshape(D, SPLIT, HID_DEV)
    up_w_split = up_weight.astype(jnp.float32).reshape(D, SPLIT, HID_DEV)
    pieces = jnp.einsum("sjh,djh->jsd", gate_split, gate_w_split, precision=highest)
    pieces = pieces + jnp.einsum("sjh,djh->jsd", up_split, up_w_split, precision=highest)
    pieces = lax.optimization_barrier(pieces.astype(jnp.bfloat16))
    partial_value = jnp.sum(pieces.astype(jnp.float32), axis=0)
    return partial_value, gate_term


def reference(out_grad, routing_weight, expert_ids, slot_index, w_gate, w_up, w_down, pre_act):
    slots_per = N_GROUP * CAP
    slot_total = EXPERTS * slots_per
    source = (jnp.arange(TOKENS, dtype=jnp.int32) // BLOCK)[:, None]
    position = expert_ids * slots_per + source * CAP + slot_index
    flat_pos = position.reshape(-1)
    repeated = jnp.repeat(out_grad, TOPK, axis=0)
    buffer_rows = jnp.zeros((slot_total, D), jnp.bfloat16).at[flat_pos].set(repeated)
    buffer_weight = jnp.zeros((slot_total,), jnp.float32).at[flat_pos].set(routing_weight.reshape(-1).astype(jnp.float32))

    def one_expert(expert):
        first_row = expert * slots_per
        token_rows = lax.dynamic_slice_in_dim(buffer_rows, first_row, slots_per, 0)
        weight = lax.dynamic_slice_in_dim(buffer_weight, first_row, slots_per, 0)
        column = expert * FF
        gate_weight = lax.dynamic_slice_in_dim(w_gate, column, FF, 1)
        up_weight = lax.dynamic_slice_in_dim(w_up, column, FF, 1)
        down_weight = lax.dynamic_slice_in_dim(w_down, column, FF, 0)
        saved_pre = lax.dynamic_slice_in_dim(pre_act, column, FF, 2)
        return expert_backward(token_rows, weight, gate_weight, up_weight, down_weight, saved_pre)

    partials, gate_terms = lax.map(one_expert, jnp.arange(EXPERTS, dtype=jnp.int32))
    partials = partials.reshape(slot_total, D)
    gate_terms = gate_terms.reshape(slot_total)
    grad_rows = jnp.sum(partials[position], axis=1)
    grad_gate = gate_terms[position]
    return grad_rows.astype(jnp.bfloat16), grad_gate
```

```python
import functools
import jax
import jax.numpy as jnp
from jax import lax
from jax.experimental import pallas as pl
from jax.experimental.pallas import tpu as pltpu
from jax.sharding import PartitionSpec as P

MESH = pl.DeviceIdType.MESH
F32 = jnp.float32
BF16 = jnp.bfloat16
SPLIT = 8
ROWS = 32
META = 64
NT = (((1,), (1,)), ((), ()))
TN = (((0,), (0,)), ((), ()))


def kernel(
    groups, experts, cap,
    grad_ref, weight_ref, ids_ref, slot_ref, wg_hbm, wu_hbm, wd_hbm, pre_hbm,
    out_ref, routing_ref,
    wd_raw, wd_pad, wcat, pre, stage, block_in, block_rows, xbuf, pbuf, wbuf,
    rbuf, ybuf, dbuf, back, gcat, gate, es, eacc, er1, er2, er3, fbuf, vbuf,
    ubuf, gsr, grr, gsl, grl, fin, hbuf,
    load_sem, a_sem, ar_sem, al_sem, b_sem, c_sem, e_sem, f_sem, gr_sem, gl_sem, h_sem,
):
    my_group = lax.axis_index("group")
    my_inner = lax.axis_index("inner")
    le = lax.div(my_inner, SPLIT)
    q = lax.rem(my_inner, SPLIT)
    zp = lax.div(q, 4)
    y = lax.rem(q, 4)
    width = grad_ref.shape[1]
    part = width // SPLIT
    lanes = xbuf.shape[2]
    last = lanes - 128
    half = experts // 2
    slots = groups * cap

    def slot_of(dz, dy):
        return lax.rem(zp + dz, 2) * 4 + lax.rem(y + dy + 4, 4)

    def in_block(index):
        return (my_group, le * SPLIT + index)

    def in_ring(step):
        return (my_group, lax.rem(le + step + experts, experts) * SPLIT + q)

    def in_group(step):
        return (lax.rem(my_group + step, groups), my_inner)

    over_z = in_block(slot_of(1, 0))
    over_up = in_block(slot_of(0, 1))
    over_down = in_block(slot_of(0, -1))
    right, left = in_ring(1), in_ring(-1)

    def send(src, dst, sems, index, target):
        copy = pltpu.make_async_remote_copy(
            src_ref=src, dst_ref=dst, send_sem=sems.at[0, index],
            recv_sem=sems.at[1, index], device_id=target, device_id_type=MESH,
        )
        copy.start()
        started.append(copy)
        return copy

    started = []
    loads = [
        pltpu.make_async_copy(wd_hbm, wd_raw, load_sem.at[0]),
        pltpu.make_async_copy(wg_hbm, wcat.at[pl.ds(0, width), pl.ds(0, 128)], load_sem.at[1]),
        pltpu.make_async_copy(wu_hbm, wcat.at[pl.ds(0, width), pl.ds(128, 128)], load_sem.at[2]),
        pltpu.make_async_copy(pre_hbm, pre, load_sem.at[3]),
    ]
    for load in loads:
        load.start()

    barrier = pltpu.get_barrier_semaphore()
    partners = [in_block(lax.rem(q + d, SPLIT)) for d in range(1, SPLIT)]
    partners += [right, left] + [in_group(d) for d in range(1, groups)]
    for partner in partners:
        pl.semaphore_signal(barrier, inc=1, device_id=partner, device_id_type=MESH)

    lane2 = lax.broadcasted_iota(jnp.int32, (2, 128), 1)
    ids = ids_ref[...]
    local = lax.rem(ids, experts).astype(F32)
    row = (lax.div(ids, experts) * ROWS + slot_ref[...]).astype(F32)
    weight = weight_ref[...].astype(F32)
    meta = jnp.zeros((2, 128), F32)
    for k in range(8):
        for at, values in ((0, local), (8, row), (16, weight)):
            meta = jnp.where(lane2 == META + at + k, values[:, k : k + 1], meta)
    tokens = grad_ref[...].astype(F32)
    for b in range(SPLIT):
        base = part * b // 128 * 128
        cut = tokens[:, base : base + lanes]
        if part * b != base:
            cut = pltpu.roll(cut, lanes - (part * b - base), 1)
        stage[b, :, 0:last] = cut[:, 0:last]
        stage[b, :, last:lanes] = jnp.where(lane2 < META, cut[:, last:lanes], meta)
    block_in[q] = stage[q]

    pl.semaphore_wait(barrier, len(partners))

    copies = []
    for d in range(1, SPLIT):
        target = lax.rem(q + d, SPLIT)
        copies.append(send(stage.at[target], block_in.at[q], a_sem, d - 1, in_block(target)))
    wcat[width:, :] = jnp.zeros((wcat.shape[0] - width, 256), BF16)
    for copy in copies:
        copy.wait_recv()
    for b in range(SPLIT):
        block_rows[2 * b : 2 * b + 2, :] = block_in[b]
    xbuf[le] = block_rows[...].astype(BF16)

    def go_right(k):
        at = lax.rem(le - (k - 1) + experts, experts)
        return send(xbuf.at[at], xbuf.at[at], ar_sem, k - 1, right)

    def go_left(k):
        at = lax.rem(le + (k - 1), experts)
        return send(xbuf.at[at], xbuf.at[at], al_sem, k - 1, left)

    lane_key = lax.broadcasted_iota(jnp.int32, (16, groups * ROWS), 1).astype(F32)
    my_local = le.astype(F32)

    def place(at):
        found = xbuf[at, :, last:lanes].astype(F32)
        key = jnp.where(found == my_local, pltpu.roll(found, 120, 1), -1.0)
        scale = pltpu.roll(found, 112, 1)
        ones = jnp.zeros(lane_key.shape, F32)
        scaled = jnp.zeros(lane_key.shape, F32)
        for k in range(8):
            hit = key[:, META + k : META + k + 1] == lane_key
            ones = jnp.where(hit, 1.0, ones)
            scaled = jnp.where(hit, scale[:, META + k : META + k + 1], scaled)
        pbuf[at] = ones.astype(BF16)
        wbuf[at] = scaled.astype(BF16)

    lane_wd = lax.broadcasted_iota(jnp.int32, (wd_raw.shape[0], lanes), 1)

    def pad_down(b):
        base = part * b // 128 * 128
        cut = wd_raw[:, base : base + lanes].astype(F32)
        if part * b != base:
            cut = pltpu.roll(cut, lanes - (part * b - base), 1)
        wd_pad[b] = jnp.where(lane_wd < part, cut, 0.0).astype(BF16)

    to_right = go_right(1)
    to_left = go_left(1) if half > 1 else None
    place(le)
    loads[0].wait()
    todo = list(range(SPLIT))
    for k in range(1, half + 1):
        to_right.wait_recv()
        if k < half:
            to_right = go_right(k + 1)
            to_left.wait_recv()
            if k < half - 1:
                to_left = go_left(k + 1)
        place(lax.rem(le - k + experts, experts))
        if k < half:
            place(lax.rem(le + k, experts))
            if todo:
                pad_down(todo.pop(0))
    rows = lax.dot_general(
        pbuf[...].reshape(experts * 16, groups * ROWS),
        xbuf[...].reshape(experts * 16, lanes),
        TN, preferred_element_type=F32,
    )
    rbuf[...] = rows.astype(BF16).reshape(rbuf.shape)

    copies = []
    for d in range(1, groups):
        target = lax.rem(my_group + d, groups)
        copies.append(send(rbuf.at[target], ybuf.at[my_group], b_sem, d - 1, in_group(d)))
    ybuf[my_group] = rbuf[my_group]
    while todo:
        pad_down(todo.pop(0))
    for copy in copies:
        copy.wait_recv()
    dense = [ybuf[s].astype(F32)[0:cap] for s in range(groups)]
    dbuf[q] = jnp.concatenate(dense, axis=0).astype(BF16)

    third = slots // 3

    def add_back(dz, dy):
        at = slot_of(dz, dy)
        back[...] += lax.dot_general(dbuf[at], wd_pad[at], NT, preferred_element_type=F32)

    def pass_on(index, dz, dy, target, cut=None):
        view = dbuf.at[slot_of(dz, dy)]
        if cut is not None:
            view = view.at[pl.ds(cut * third, third)]
        return send(view, view, c_sem, index, target)

    z1 = pass_on(0, 0, 0, over_z)
    u1 = pass_on(1, 0, 0, over_up)
    d1 = pass_on(2, 0, 0, over_down)
    back[...] = jnp.zeros(back.shape, F32)
    add_back(0, 0)
    d1.wait_recv()
    z2 = pass_on(3, 0, 1, over_z)
    d2 = pass_on(5, 0, 1, over_down)
    z1.wait_recv()
    u2 = pass_on(4, 1, 0, over_up)
    u1.wait_recv()
    for dz, dy in ((0, 1), (1, 0), (0, -1)):
        add_back(dz, dy)
    d2.wait_recv()
    z3 = pass_on(6, 0, 2, over_z, 0)
    z2.wait_recv()
    d3 = pass_on(8, 1, 1, over_down, 1)
    u2.wait_recv()
    u3 = pass_on(7, 1, -1, over_up, 2)
    for dz, dy in ((0, 2), (1, 1), (1, -1)):
        add_back(dz, dy)
    for load in loads[1:]:
        load.wait()
    z3.wait_recv()
    d3.wait_recv()
    u3.wait_recv()
    add_back(1, 2)

    proj = back[...]
    pre_gate = pre[0].astype(F32)
    pre_up = pre[1].astype(F32)
    sig = jax.nn.sigmoid(pre_gate)
    swish = pre_gate * sig
    gcat[:, 0:128] = (proj * pre_up * sig * (1.0 + pre_gate * (1.0 - sig))).astype(BF16)
    gcat[:, 128:256] = (proj * swish).astype(BF16)
    gate[...] = jnp.broadcast_to(
        jnp.sum(swish * pre_up * proj, axis=1, keepdims=True), gate.shape
    )
    lane_tile = lax.broadcasted_iota(jnp.int32, gate.shape, 1)

    def piece(dz, dy, out, at):
        start = pl.multiple_of(slot_of(dz, dy) * part, 64)
        value = lax.dot_general(
            gcat[...], wcat[pl.ds(start, lanes), :], NT, preferred_element_type=F32
        )
        out[at, :, 0:last] = value[:, 0:last].astype(out.dtype)
        out[at, :, last:lanes] = jnp.where(
            lane_tile < META, value[:, last:lanes], gate[...]
        ).astype(out.dtype)

    piece(1, 2, es, 0)
    z1 = send(es.at[0, pl.ds(0, third)], er1.at[0], e_sem, 0, over_z)
    u1 = send(es.at[0, pl.ds(third, third)], er1.at[1], e_sem, 1, over_up)
    d1 = send(es.at[0, pl.ds(2 * third, third)], er1.at[2], e_sem, 2, over_down)

    def joined(acc, at, arrived, cut):
        piece_at = eacc[acc]
        own = piece_at[cut * third : (cut + 1) * third] + arrived.astype(F32)
        es[at] = piece_at.astype(BF16)
        es[at, cut * third : (cut + 1) * third] = own.astype(BF16)

    piece(1, 1, eacc, 0)
    u1.wait_recv()
    joined(0, 1, er1[1], 1)
    z2 = send(es.at[1], er2.at[0], e_sem, 3, over_z)
    piece(0, 2, eacc, 0)
    z1.wait_recv()
    joined(0, 2, er1[0], 0)
    u2 = send(es.at[2], er2.at[1], e_sem, 4, over_up)
    piece(1, -1, eacc, 0)
    d1.wait_recv()
    joined(0, 3, er1[2], 2)
    d2 = send(es.at[3], er2.at[2], e_sem, 5, over_down)
    piece(0, -1, es, 6)
    d3 = send(es.at[6], er3.at[2], e_sem, 8, over_down)
    piece(1, 0, eacc, 0)
    piece(0, 1, eacc, 1)
    d2.wait_recv()
    es[4] = (eacc[0] + er2[2].astype(F32)).astype(BF16)
    z3 = send(es.at[4], er3.at[0], e_sem, 6, over_z)
    z2.wait_recv()
    u2.wait_recv()
    es[5] = (eacc[1] + er2[0].astype(F32) + er2[1].astype(F32)).astype(BF16)
    u3 = send(es.at[5], er3.at[1], e_sem, 7, over_up)
    piece(0, 0, eacc, 2)
    d3.wait_recv()
    z3.wait_recv()
    u3.wait_recv()
    blank = jnp.zeros((ROWS - cap, lanes), F32)
    summed = (
        eacc[2] + er3[0].astype(F32) + er3[1].astype(F32) + er3[2].astype(F32)
    )
    for s in range(groups):
        fbuf[s] = jnp.concatenate(
            [summed[s * cap : (s + 1) * cap], blank], axis=0
        ).astype(BF16)

    copies = []
    for d in range(1, groups):
        target = lax.rem(my_group + d, groups)
        copies.append(send(fbuf.at[target], vbuf.at[my_group], f_sem, d - 1, in_group(d)))
    vbuf[my_group] = fbuf[my_group]
    for copy in copies:
        copy.wait_recv()

    arrived = vbuf[...].reshape(groups * ROWS, lanes)
    ubuf[...] = lax.dot_general(
        wbuf[...].reshape(experts * 16, groups * ROWS), arrived,
        (((1,), (0,)), ((), ())), preferred_element_type=F32,
    ).reshape(ubuf.shape)
    row_group = lax.div(lax.broadcasted_iota(jnp.int32, (groups * ROWS, 128), 0), ROWS)
    lane_group = lax.broadcasted_iota(jnp.int32, (groups * ROWS, 128), 1) - META
    spread = jnp.where(
        row_group == lane_group, arrived[:, last:lanes].astype(F32), 0.0
    ).astype(BF16)
    terms = lax.dot_general(
        pbuf[...].reshape(experts * 16, groups * ROWS), spread,
        (((1,), (0,)), ((), ())), preferred_element_type=F32,
    )
    found = xbuf[...].reshape(experts * 16, lanes)[:, last:lanes].astype(F32)
    key = jnp.where(found == my_local, pltpu.roll(found, 120, 1), -1.0)
    of_group = jnp.floor(key * (1.0 / ROWS))
    routed = jnp.zeros(found.shape, F32)
    for g in range(groups):
        routed = jnp.where(of_group == g, terms[:, META + g : META + g + 1], routed)
    lane_all = lax.broadcasted_iota(jnp.int32, found.shape, 1)
    mine = ubuf[...].reshape(experts * 16, lanes)[:, last:lanes]
    ubuf[:, :, last:lanes] = jnp.where(lane_all < META, mine, routed).reshape(
        experts, 16, 128
    )

    to_right = to_left = None
    for k in range(1, half + 1):
        value = ubuf[lax.rem(le + half + 1 - k, experts)]
        if to_right is not None:
            to_right.wait_recv()
            value = value + grr[k - 2].astype(F32)
        gsr[k - 1] = value.astype(BF16)
        to_right = send(gsr.at[k - 1], grr.at[k - 1], gr_sem, k - 1, right)
        if k < half:
            value = ubuf[lax.rem(le - (half - k) + experts, experts)]
            if to_left is not None:
                to_left.wait_recv()
                value = value + grl[k - 2].astype(F32)
            gsl[k - 1] = value.astype(BF16)
            to_left = send(gsl.at[k - 1], grl.at[k - 1], gl_sem, k - 1, left)
    value = ubuf[le]
    if to_left is not None:
        to_left.wait_recv()
        value = value + grl[half - 2].astype(F32)
    to_right.wait_recv()
    value = value + grr[half - 1].astype(F32)

    block_rows[...] = value
    for b in range(SPLIT):
        fin[b] = block_rows[2 * b : 2 * b + 2, :]
    hbuf[q] = fin[q]
    copies = []
    for d in range(1, SPLIT):
        target = lax.rem(q + d, SPLIT)
        copies.append(send(fin.at[target], hbuf.at[q], h_sem, d - 1, in_block(target)))
    for copy in copies:
        copy.wait_recv()
    for m in range(SPLIT // 2):
        even = hbuf[2 * m]
        odd = pltpu.roll(hbuf[2 * m + 1], META, 1)
        base = 2 * part * m
        out_ref[:, base : base + last] = even[:, 0:last].astype(BF16)
        out_ref[:, base + last : base + lanes] = jnp.where(
            lane2 < META, even[:, last:lanes], odd[:, 0:128]
        ).astype(BF16)
        out_ref[:, base + lanes : base + 2 * part] = odd[:, 128:lanes].astype(BF16)
    routing_ref[...] = pltpu.roll(hbuf[0][:, last:lanes], 128 - META, 1)[:, 0:8]
    for copy in started:
        copy.wait_send()


def on_device(out_grad, routing_weight, expert_ids, slot_index, w_gate, w_up, w_down, pre_act):
    groups = lax.axis_size("group")
    experts = lax.axis_size("inner") // SPLIT
    cap = pre_act.shape[1] // groups
    width = out_grad.shape[1]
    lanes = -(-(width // SPLIT) // 128) * 128
    slots = groups * cap
    hidden = w_down.shape[0]
    half = experts // 2
    vmem = pltpu.VMEM
    dma = pltpu.SemaphoreType.DMA
    scratch = [
        vmem((hidden, width), BF16),
        vmem((SPLIT, hidden, lanes), BF16),
        vmem((width // SPLIT * (SPLIT - 1) + lanes, 256), BF16),
        vmem((2, slots, hidden), BF16),
        vmem((SPLIT, 2, lanes), F32),
        vmem((SPLIT, 2, lanes), F32),
        vmem((16, lanes), F32),
        vmem((experts, 16, lanes), BF16),
        vmem((experts, 16, groups * ROWS), BF16),
        vmem((experts, 16, groups * ROWS), BF16),
        vmem((groups, ROWS, lanes), BF16),
        vmem((groups, ROWS, lanes), BF16),
        vmem((SPLIT, slots, lanes), BF16),
        vmem((slots, hidden), F32),
        vmem((slots, 256), BF16),
        vmem((slots, 128), F32),
        vmem((7, slots, lanes), BF16),
        vmem((3, slots, lanes), F32),
        vmem((3, slots // 3, lanes), BF16),
        vmem((3, slots, lanes), BF16),
        vmem((3, slots, lanes), BF16),
        vmem((groups, ROWS, lanes), BF16),
        vmem((groups, ROWS, lanes), BF16),
        vmem((experts, 16, lanes), F32),
        vmem((half, 16, lanes), BF16),
        vmem((half, 16, lanes), BF16),
        vmem((half, 16, lanes), BF16),
        vmem((half, 16, lanes), BF16),
        vmem((SPLIT, 2, lanes), F32),
        vmem((SPLIT, 2, lanes), F32),
        dma((4,)),
        dma((2, SPLIT)),
        dma((2, half)),
        dma((2, half)),
        dma((2, groups)),
        dma((2, 9)),
        dma((2, 9)),
        dma((2, groups)),
        dma((2, half)),
        dma((2, half)),
        dma((2, SPLIT)),
    ]
    in_vmem = pl.BlockSpec(memory_space=pltpu.VMEM)
    anywhere = pl.BlockSpec(memory_space=pl.ANY)
    return pl.pallas_call(
        functools.partial(kernel, groups, experts, cap),
        out_shape=(
            jax.ShapeDtypeStruct(out_grad.shape, BF16),
            jax.ShapeDtypeStruct(expert_ids.shape, F32),
        ),
        in_specs=[in_vmem] * 4 + [anywhere] * 4,
        out_specs=(in_vmem, in_vmem),
        scratch_shapes=scratch,
        compiler_params=pltpu.CompilerParams(
            collective_id=0, has_side_effects=True, vmem_limit_bytes=40 * 2**20
        ),
        name="routed_backward",
    )(out_grad, routing_weight, expert_ids, slot_index, w_gate, w_up, w_down, pre_act)


def solution(mesh):
    token = P(("group", "inner"), None)
    in_specs = (
        token, token, token, token,
        P(None, ("group", "inner")),
        P(None, ("group", "inner")),
        P(("group", "inner"), None),
        P(None, None, ("group", "inner")),
    )
    return jax.shard_map(
        on_device, mesh=mesh, in_specs=in_specs, out_specs=(token, token), check_vma=False
    )
```

```python
import functools
import jax
import jax.numpy as jnp
from jax import lax
from jax.experimental import pallas as pl
from jax.experimental.pallas import tpu as pltpu
from jax.sharding import PartitionSpec as P

MESH = pl.DeviceIdType.MESH
F32 = jnp.float32
BF16 = jnp.bfloat16
SPLIT = 8
ROWS = 32
META = 64
NT = (((1,), (1,)), ((), ()))
TN = (((0,), (0,)), ((), ()))


def kernel(
    groups, experts, cap,
    grad_hbm, weight_hbm, ids_hbm, slot_hbm, wg_hbm, wu_hbm, wd_hbm, pre_hbm,
    out_ref, routing_ref,
    grad_ref, weight_ref, ids_ref, slot_ref, wd_raw, wd_pad, wcat, pre, stage, block_in, block_rows, xbuf, pbuf, wbuf,
    rbuf, ybuf, dbuf, back, gcat, gate, es, eacc, er1, er2, er3, fbuf, vbuf,
    ubuf, ubf, gsr, grr, gsl, grl, gnr, gnl, fin, hbuf,
    load_sem, a_sem, ar_sem, al_sem, anr_sem, anl_sem, b_sem, c_sem, e_sem, f_sem,
    gr_sem, gl_sem, gnr_sem, gnl_sem, h_sem,
):
    my_group = lax.axis_index("group")
    my_inner = lax.axis_index("inner")
    le = lax.div(my_inner, SPLIT)
    q = lax.rem(my_inner, SPLIT)
    zp = lax.div(q, 4)
    y = lax.rem(q, 4)
    width = grad_ref.shape[1]
    part = width // SPLIT
    lanes = xbuf.shape[2]
    last = lanes - 128
    half = experts // 4
    slots = groups * cap

    def slot_of(dz, dy):
        return lax.rem(zp + dz, 2) * 4 + lax.rem(y + dy + 4, 4)

    def in_block(index):
        return (my_group, le * SPLIT + index)

    def in_ring(step):
        return (my_group, lax.rem(le + step + experts, experts) * SPLIT + q)

    def in_group(step):
        return (lax.rem(my_group + step, groups), my_inner)

    over_z = in_block(slot_of(1, 0))
    over_up = in_block(slot_of(0, 1))
    over_down = in_block(slot_of(0, -1))
    right, left = in_ring(2), in_ring(-2)
    next_right, next_left = in_ring(1), in_ring(-1)

    def send(src, dst, sems, index, target):
        copy = pltpu.make_async_remote_copy(
            src_ref=src, dst_ref=dst, send_sem=sems.at[0, index],
            recv_sem=sems.at[1, index], device_id=target, device_id_type=MESH,
        )
        copy.start()
        started.append(copy)
        return copy

    started = []
    loads = [
        pltpu.make_async_copy(wd_hbm, wd_raw, load_sem.at[0]),
        pltpu.make_async_copy(wg_hbm, wcat.at[pl.ds(0, width), pl.ds(0, 128)], load_sem.at[1]),
        pltpu.make_async_copy(wu_hbm, wcat.at[pl.ds(0, width), pl.ds(128, 128)], load_sem.at[2]),
        pltpu.make_async_copy(pre_hbm, pre, load_sem.at[3]),
    ]
    small = [
        pltpu.make_async_copy(grad_hbm, grad_ref, load_sem.at[4]),
        pltpu.make_async_copy(weight_hbm, weight_ref, load_sem.at[5]),
        pltpu.make_async_copy(ids_hbm, ids_ref, load_sem.at[6]),
        pltpu.make_async_copy(slot_hbm, slot_ref, load_sem.at[7]),
    ]
    for load in small + loads:
        load.start()

    barrier = pltpu.get_barrier_semaphore()
    partners = [in_block(lax.rem(q + d, SPLIT)) for d in range(1, SPLIT)]
    partners += [right, left, next_right, next_left] + [in_group(d) for d in range(1, groups)]
    for partner in partners:
        pl.semaphore_signal(barrier, inc=1, device_id=partner, device_id_type=MESH)

    for load in small:
        load.wait()
    lane2 = lax.broadcasted_iota(jnp.int32, (2, 128), 1)
    ids = ids_ref[...]
    local = lax.rem(ids, experts).astype(F32)
    row = (lax.div(ids, experts) * ROWS + slot_ref[...]).astype(F32)
    weight = weight_ref[...].astype(F32)
    meta = jnp.zeros((2, 128), F32)
    for k in range(8):
        for at, values in ((0, local), (8, row), (16, weight)):
            meta = jnp.where(lane2 == META + at + k, values[:, k : k + 1], meta)
    tokens = grad_ref[...].astype(F32)
    for b in range(SPLIT):
        base = part * b // 128 * 128
        cut = tokens[:, base : base + lanes]
        if part * b != base:
            cut = pltpu.roll(cut, lanes - (part * b - base), 1)
        stage[b, :, 0:last] = cut[:, 0:last]
        stage[b, :, last:lanes] = jnp.where(lane2 < META, cut[:, last:lanes], meta)
    block_in[q] = stage[q]

    pl.semaphore_wait(barrier, len(partners))

    copies = []
    for d in range(1, SPLIT):
        target = lax.rem(q + d, SPLIT)
        copies.append(send(stage.at[target], block_in.at[q], a_sem, d - 1, in_block(target)))
    wcat[width:, :] = jnp.zeros((wcat.shape[0] - width, 256), BF16)
    for copy in copies:
        copy.wait_recv()
    for b in range(SPLIT):
        block_rows[2 * b : 2 * b + 2, :] = block_in[b]
    xbuf[le] = block_rows[...].astype(BF16)

    def block(step):
        return lax.rem(le + step + experts, experts)

    def go(step, sems, index, target):
        return send(xbuf.at[block(step)], xbuf.at[block(step)], sems, index, target)

    lane_key = lax.broadcasted_iota(jnp.int32, (16, groups * ROWS), 1).astype(F32)
    my_local = le.astype(F32)

    def place(at):
        found = xbuf[at, :, last:lanes].astype(F32)
        key = jnp.where(found == my_local, pltpu.roll(found, 120, 1), -1.0)
        scale = pltpu.roll(found, 112, 1)
        ones = jnp.zeros(lane_key.shape, F32)
        scaled = jnp.zeros(lane_key.shape, F32)
        for k in range(8):
            hit = key[:, META + k : META + k + 1] == lane_key
            ones = jnp.where(hit, 1.0, ones)
            scaled = jnp.where(hit, scale[:, META + k : META + k + 1], scaled)
        pbuf[at] = ones.astype(BF16)
        wbuf[at] = scaled.astype(BF16)

    lane_wd = lax.broadcasted_iota(jnp.int32, (wd_raw.shape[0], lanes), 1)

    def pad_down(b):
        base = part * b // 128 * 128
        cut = wd_raw[:, base : base + lanes].astype(F32)
        if part * b != base:
            cut = pltpu.roll(cut, lanes - (part * b - base), 1)
        wd_pad[b] = jnp.where(lane_wd < part, cut, 0.0).astype(BF16)

    to_right = go(0, ar_sem, 0, right)
    to_left = go(0, al_sem, 0, left) if half > 1 else None
    near_right = go(0, anr_sem, 0, next_right)
    near_left = go(0, anl_sem, 0, next_left)
    place(le)
    loads[0].wait()
    todo = list(range(SPLIT))
    for k in range(1, half + 1):
        last_right, last_left = near_right, near_left
        if k < half:
            to_left.wait_recv()
            if k < half - 1:
                to_left = go(2 * k, al_sem, k, left)
            near_left = go(2 * k, anl_sem, k, next_left)
        to_right.wait_recv()
        if k < half:
            to_right = go(-2 * k, ar_sem, k, right)
            near_right = go(-2 * k, anr_sem, k, next_right)
            place(block(2 * k))
        last_right.wait_recv()
        last_left.wait_recv()
        for step in (1 - 2 * k, 2 * k - 1, -2 * k):
            place(block(step))
        for _ in range(2):
            if todo and k < half:
                pad_down(todo.pop(0))
    rows = lax.dot_general(
        pbuf[...].reshape(experts * 16, groups * ROWS),
        xbuf[...].reshape(experts * 16, lanes),
        TN, preferred_element_type=F32,
    )
    rbuf[...] = rows.astype(BF16).reshape(rbuf.shape)

    copies = []
    for d in range(1, groups):
        target = lax.rem(my_group + d, groups)
        copies.append(send(rbuf.at[target], ybuf.at[my_group], b_sem, d - 1, in_group(d)))
    ybuf[my_group] = rbuf[my_group]
    while todo:
        pad_down(todo.pop(0))
    for copy in copies:
        copy.wait_recv()
    dense = [ybuf[s].astype(F32)[0:cap] for s in range(groups)]
    dbuf[q] = jnp.concatenate(dense, axis=0).astype(BF16)

    third = slots // 3

    def add_back(dz, dy):
        at = slot_of(dz, dy)
        back[...] += lax.dot_general(dbuf[at], wd_pad[at], NT, preferred_element_type=F32)

    def pass_on(index, dz, dy, target, cut=None):
        view = dbuf.at[slot_of(dz, dy)]
        if cut is not None:
            view = view.at[pl.ds(cut * third, third)]
        return send(view, view, c_sem, index, target)

    z1 = pass_on(0, 0, 0, over_z)
    u1 = pass_on(1, 0, 0, over_up)
    d1 = pass_on(2, 0, 0, over_down)
    back[...] = jnp.zeros(back.shape, F32)
    add_back(0, 0)
    d1.wait_recv()
    z2 = pass_on(3, 0, 1, over_z)
    d2 = pass_on(5, 0, 1, over_down)
    z1.wait_recv()
    u2 = pass_on(4, 1, 0, over_up)
    u1.wait_recv()
    for dz, dy in ((0, 1), (1, 0), (0, -1)):
        add_back(dz, dy)
    d2.wait_recv()
    z3 = pass_on(6, 0, 2, over_z, 0)
    z2.wait_recv()
    d3 = pass_on(8, 1, 1, over_down, 1)
    u2.wait_recv()
    u3 = pass_on(7, 1, -1, over_up, 2)
    for dz, dy in ((0, 2), (1, 1), (1, -1)):
        add_back(dz, dy)
    for load in loads[1:]:
        load.wait()
    z3.wait_recv()
    d3.wait_recv()
    u3.wait_recv()
    add_back(1, 2)

    proj = back[...]
    pre_gate = pre[0].astype(F32)
    pre_up = pre[1].astype(F32)
    sig = jax.nn.sigmoid(pre_gate)
    swish = pre_gate * sig
    gcat[:, 0:128] = (proj * pre_up * sig * (1.0 + pre_gate * (1.0 - sig))).astype(BF16)
    gcat[:, 128:256] = (proj * swish).astype(BF16)
    gate[...] = jnp.broadcast_to(
        jnp.sum(swish * pre_up * proj, axis=1, keepdims=True), gate.shape
    )
    lane_tile = lax.broadcasted_iota(jnp.int32, gate.shape, 1)

    def piece(dz, dy, out, at):
        start = pl.multiple_of(slot_of(dz, dy) * part, 64)
        value = lax.dot_general(
            gcat[...], wcat[pl.ds(start, lanes), :], NT, preferred_element_type=F32
        )
        out[at, :, 0:last] = value[:, 0:last].astype(out.dtype)
        out[at, :, last:lanes] = jnp.where(
            lane_tile < META, value[:, last:lanes], gate[...]
        ).astype(out.dtype)

    piece(1, 2, es, 0)
    z1 = send(es.at[0, pl.ds(0, third)], er1.at[0], e_sem, 0, over_z)
    u1 = send(es.at[0, pl.ds(third, third)], er1.at[1], e_sem, 1, over_up)
    d1 = send(es.at[0, pl.ds(2 * third, third)], er1.at[2], e_sem, 2, over_down)

    def joined(acc, at, arrived, cut):
        piece_at = eacc[acc]
        own = piece_at[cut * third : (cut + 1) * third] + arrived.astype(F32)
        es[at] = piece_at.astype(BF16)
        es[at, cut * third : (cut + 1) * third] = own.astype(BF16)

    piece(1, 1, eacc, 0)
    u1.wait_recv()
    joined(0, 1, er1[1], 1)
    z2 = send(es.at[1], er2.at[0], e_sem, 3, over_z)
    piece(0, 2, eacc, 0)
    z1.wait_recv()
    joined(0, 2, er1[0], 0)
    u2 = send(es.at[2], er2.at[1], e_sem, 4, over_up)
    piece(1, -1, eacc, 0)
    d1.wait_recv()
    joined(0, 3, er1[2], 2)
    d2 = send(es.at[3], er2.at[2], e_sem, 5, over_down)
    piece(0, -1, es, 6)
    d3 = send(es.at[6], er3.at[2], e_sem, 8, over_down)
    piece(1, 0, eacc, 0)
    piece(0, 1, eacc, 1)
    d2.wait_recv()
    es[4] = (eacc[0] + er2[2].astype(F32)).astype(BF16)
    z3 = send(es.at[4], er3.at[0], e_sem, 6, over_z)
    z2.wait_recv()
    u2.wait_recv()
    es[5] = (eacc[1] + er2[0].astype(F32) + er2[1].astype(F32)).astype(BF16)
    u3 = send(es.at[5], er3.at[1], e_sem, 7, over_up)
    piece(0, 0, eacc, 2)
    d3.wait_recv()
    z3.wait_recv()
    u3.wait_recv()
    blank = jnp.zeros((ROWS - cap, lanes), F32)
    summed = (
        eacc[2] + er3[0].astype(F32) + er3[1].astype(F32) + er3[2].astype(F32)
    )
    for s in range(groups):
        fbuf[s] = jnp.concatenate(
            [summed[s * cap : (s + 1) * cap], blank], axis=0
        ).astype(BF16)

    copies = []
    for d in range(1, groups):
        target = lax.rem(my_group + d, groups)
        copies.append(send(fbuf.at[target], vbuf.at[my_group], f_sem, d - 1, in_group(d)))
    vbuf[my_group] = fbuf[my_group]
    for copy in copies:
        copy.wait_recv()

    arrived = vbuf[...].reshape(groups * ROWS, lanes)
    ubuf[...] = lax.dot_general(
        wbuf[...].reshape(experts * 16, groups * ROWS), arrived,
        (((1,), (0,)), ((), ())), preferred_element_type=F32,
    ).reshape(ubuf.shape)
    row_group = lax.div(lax.broadcasted_iota(jnp.int32, (groups * ROWS, 128), 0), ROWS)
    lane_group = lax.broadcasted_iota(jnp.int32, (groups * ROWS, 128), 1) - META
    spread = jnp.where(
        row_group == lane_group, arrived[:, last:lanes].astype(F32), 0.0
    ).astype(BF16)
    terms = lax.dot_general(
        pbuf[...].reshape(experts * 16, groups * ROWS), spread,
        (((1,), (0,)), ((), ())), preferred_element_type=F32,
    )
    found = xbuf[...].reshape(experts * 16, lanes)[:, last:lanes].astype(F32)
    key = jnp.where(found == my_local, pltpu.roll(found, 120, 1), -1.0)
    of_group = jnp.floor(key * (1.0 / ROWS))
    routed = jnp.zeros(found.shape, F32)
    for g in range(groups):
        routed = jnp.where(of_group == g, terms[:, META + g : META + g + 1], routed)
    lane_all = lax.broadcasted_iota(jnp.int32, found.shape, 1)
    mine = ubuf[...].reshape(experts * 16, lanes)[:, last:lanes]
    ubuf[:, :, last:lanes] = jnp.where(lane_all < META, mine, routed).reshape(
        experts, 16, 128
    )

    ubf[...] = ubuf[...].astype(BF16)
    to_right = send(ubf.at[block(2 * half)], grr.at[0], gr_sem, 0, right)
    to_left = None
    near_right, near_left = [None] * half, [None] * half
    for k in range(half - 1, -1, -1):
        near_left[k] = send(ubf.at[block(-1 - 2 * k)], gnl.at[k], gnl_sem, k, next_left)
        near_right[k] = send(ubf.at[block(1 + 2 * k)], gnr.at[k], gnr_sem, k, next_right)
    for k in range(half - 1, 0, -1):
        value = ubuf[block(-2 * k)]
        near_left[k].wait_recv()
        value = value + gnl[k].astype(F32)
        if to_left is not None:
            to_left.wait_recv()
            value = value + grl[half - 2 - k].astype(F32)
        gsl[half - 1 - k] = value.astype(BF16)
        to_left = send(gsl.at[half - 1 - k], grl.at[half - 1 - k], gl_sem, half - 1 - k, left)
        value = ubuf[block(2 * k)]
        near_right[k].wait_recv()
        value = value + gnr[k].astype(F32)
        to_right.wait_recv()
        value = value + grr[half - 1 - k].astype(F32)
        gsr[half - 1 - k] = value.astype(BF16)
        to_right = send(gsr.at[half - 1 - k], grr.at[half - k], gr_sem, half - k, right)
    near_right[0].wait_recv()
    near_left[0].wait_recv()
    value = ubuf[le] + gnr[0].astype(F32) + gnl[0].astype(F32)
    if to_left is not None:
        to_left.wait_recv()
        value = value + grl[half - 2].astype(F32)
    to_right.wait_recv()
    value = value + grr[half - 1].astype(F32)

    block_rows[...] = value
    for b in range(SPLIT):
        fin[b] = block_rows[2 * b : 2 * b + 2, :]
    hbuf[q] = fin[q]
    copies = []
    for d in range(1, SPLIT):
        target = lax.rem(q + d, SPLIT)
        copies.append(send(fin.at[target], hbuf.at[q], h_sem, d - 1, in_block(target)))
    for copy in copies:
        copy.wait_recv()
    for m in range(SPLIT // 2):
        even = hbuf[2 * m]
        odd = pltpu.roll(hbuf[2 * m + 1], META, 1)
        base = 2 * part * m
        out_ref[:, base : base + last] = even[:, 0:last].astype(BF16)
        out_ref[:, base + last : base + lanes] = jnp.where(
            lane2 < META, even[:, last:lanes], odd[:, 0:128]
        ).astype(BF16)
        out_ref[:, base + lanes : base + 2 * part] = odd[:, 128:lanes].astype(BF16)
    routing_ref[...] = pltpu.roll(hbuf[0][:, last:lanes], 128 - META, 1)[:, 0:8]
    for copy in started:
        copy.wait_send()


def on_device(out_grad, routing_weight, expert_ids, slot_index, w_gate, w_up, w_down, pre_act):
    groups = lax.axis_size("group")
    experts = lax.axis_size("inner") // SPLIT
    cap = pre_act.shape[1] // groups
    width = out_grad.shape[1]
    lanes = -(-(width // SPLIT) // 128) * 128
    slots = groups * cap
    hidden = w_down.shape[0]
    half = experts // 4
    vmem = pltpu.VMEM
    dma = pltpu.SemaphoreType.DMA
    scratch = [
        vmem(out_grad.shape, BF16),
        vmem(routing_weight.shape, BF16),
        vmem(expert_ids.shape, jnp.int32),
        vmem(slot_index.shape, jnp.int32),
        vmem((hidden, width), BF16),
        vmem((SPLIT, hidden, lanes), BF16),
        vmem((width // SPLIT * (SPLIT - 1) + lanes, 256), BF16),
        vmem((2, slots, hidden), BF16),
        vmem((SPLIT, 2, lanes), F32),
        vmem((SPLIT, 2, lanes), F32),
        vmem((16, lanes), F32),
        vmem((experts, 16, lanes), BF16),
        vmem((experts, 16, groups * ROWS), BF16),
        vmem((experts, 16, groups * ROWS), BF16),
        vmem((groups, ROWS, lanes), BF16),
        vmem((groups, ROWS, lanes), BF16),
        vmem((SPLIT, slots, lanes), BF16),
        vmem((slots, hidden), F32),
        vmem((slots, 256), BF16),
        vmem((slots, 128), F32),
        vmem((7, slots, lanes), BF16),
        vmem((3, slots, lanes), F32),
        vmem((3, slots // 3, lanes), BF16),
        vmem((3, slots, lanes), BF16),
        vmem((3, slots, lanes), BF16),
        vmem((groups, ROWS, lanes), BF16),
        vmem((groups, ROWS, lanes), BF16),
        vmem((experts, 16, lanes), F32),
        vmem((experts, 16, lanes), BF16),
        vmem((half, 16, lanes), BF16),
        vmem((half, 16, lanes), BF16),
        vmem((half, 16, lanes), BF16),
        vmem((half, 16, lanes), BF16),
        vmem((half, 16, lanes), BF16),
        vmem((half, 16, lanes), BF16),
        vmem((SPLIT, 2, lanes), F32),
        vmem((SPLIT, 2, lanes), F32),
        dma((8,)),
        dma((2, SPLIT)),
        dma((2, half)),
        dma((2, half)),
        dma((2, half)),
        dma((2, half)),
        dma((2, groups)),
        dma((2, 9)),
        dma((2, 9)),
        dma((2, groups)),
        dma((2, half)),
        dma((2, half)),
        dma((2, half)),
        dma((2, half)),
        dma((2, SPLIT)),
    ]
    in_vmem = pl.BlockSpec(memory_space=pltpu.VMEM)
    anywhere = pl.BlockSpec(memory_space=pl.ANY)
    return pl.pallas_call(
        functools.partial(kernel, groups, experts, cap),
        out_shape=(
            jax.ShapeDtypeStruct(out_grad.shape, BF16),
            jax.ShapeDtypeStruct(expert_ids.shape, F32),
        ),
        in_specs=[anywhere] * 8,
        out_specs=(in_vmem, in_vmem),
        scratch_shapes=scratch,
        compiler_params=pltpu.CompilerParams(
            collective_id=0, has_side_effects=True, vmem_limit_bytes=60 * 2**20
        ),
        name="routed_backward",
    )(out_grad, routing_weight, expert_ids, slot_index, w_gate, w_up, w_down, pre_act)


def solution(mesh):
    token = P(("group", "inner"), None)
    in_specs = (
        token, token, token, token,
        P(None, ("group", "inner")),
        P(None, ("group", "inner")),
        P(("group", "inner"), None),
        P(None, None, ("group", "inner")),
    )
    return jax.shard_map(
        on_device, mesh=mesh, in_specs=in_specs, out_specs=(token, token), check_vma=False
    )
```

```python
import functools
import jax
import jax.numpy as jnp
from jax import lax
from jax.experimental import pallas as pl
from jax.experimental.pallas import tpu as pltpu
from jax.sharding import PartitionSpec as P

MESH = pl.DeviceIdType.MESH
F32 = jnp.float32
BF16 = jnp.bfloat16
SPLIT = 8
ROWS = 32
CHUNKS = 2
NT = (((1,), (1,)), ((), ()))
TN = (((0,), (0,)), ((), ()))
NN = (((1,), (0,)), ((), ()))


def kernel(
    groups, experts, cap,
    grad_hbm, weight_hbm, ids_hbm, slot_hbm, wg_hbm, wu_hbm, wd_hbm, pre_hbm,
    out_ref, routing_ref,
    grad_ref, weight_ref, ids_ref, slot_ref, wd_cols, wc, pre, stage, block_in,
    block_rows, xbuf, pbuf, wbuf, rbuf, ybuf, dbuf, bsend, brecv, back, gall, gate,
    fbuf, vbuf, ubuf, ubf, gsr, grr, gsl, grl, gnr, gnl, fin, hbuf,
    load_sem, a_sem, ar_sem, al_sem, anr_sem, anl_sem, wd_sem, wc_sem, b_sem, c_sem,
    d_sem, f_sem, gr_sem, gl_sem, gnr_sem, gnl_sem, h_sem,
):
    my_group = lax.axis_index("group")
    my_inner = lax.axis_index("inner")
    le = lax.div(my_inner, SPLIT)
    q = lax.rem(my_inner, SPLIT)
    zp = lax.div(q, 4)
    y = lax.rem(q, 4)
    odd = lax.rem(y, 2)
    width = grad_ref.shape[1]
    part = width // SPLIT
    lanes = xbuf.shape[2]
    last = lanes - 128
    half = experts // 4
    slots = groups * cap

    def window(index):
        return 2 * part * (index // 2) + last * (index % 2)

    def window_at(index):
        return 2 * part * lax.div(index, 2) + last * lax.rem(index, 2)

    def in_block(index):
        return (my_group, le * SPLIT + index)

    def in_ring(step):
        return (my_group, lax.rem(le + step + experts, experts) * SPLIT + q)

    def along_y(step):
        return in_block(zp * 4 + lax.rem(y + step, 4))

    def in_group(step, z):
        return (lax.rem(my_group + step, groups), le * SPLIT + z * 4 + y)

    right, left = in_ring(2), in_ring(-2)
    next_right, next_left = in_ring(1), in_ring(-1)

    def send(src, dst, sems, index, target):
        copy = pltpu.make_async_remote_copy(
            src_ref=src, dst_ref=dst, send_sem=sems.at[0, index],
            recv_sem=sems.at[1, index], device_id=target, device_id_type=MESH,
        )
        copy.start()
        started.append(copy)
        return copy

    started = []
    small = [
        pltpu.make_async_copy(grad_hbm, grad_ref, load_sem.at[0]),
        pltpu.make_async_copy(weight_hbm, weight_ref, load_sem.at[1]),
        pltpu.make_async_copy(ids_hbm, ids_ref, load_sem.at[2]),
        pltpu.make_async_copy(slot_hbm, slot_ref, load_sem.at[3]),
    ]
    for load in small:
        load.start()

    barrier = pltpu.get_barrier_semaphore()
    partners = [in_block(lax.rem(q + d, SPLIT)) for d in range(1, SPLIT)]
    partners += [right, left, next_right, next_left]
    partners += [in_group(d, z) for d in range(1, groups) for z in (zp, 1 - zp)]
    for partner in partners:
        pl.semaphore_signal(barrier, inc=1, device_id=partner, device_id_type=MESH)

    def down_window(z, step):
        at = window_at(z * 4 + lax.rem(y + step, 4))
        return wd_hbm.at[:, pl.ds(pl.multiple_of(at, 128), lanes)]

    def wide_window(ref, z, step):
        at = window_at(z * 4 + lax.rem(y + step, 4))
        return ref.at[pl.ds(pl.multiple_of(at, 128), lanes), :]

    def wide_at(z, which):
        return wc.at[y, z, :, pl.ds(128 * which, 128)]

    loads = [pltpu.make_async_copy(pre_hbm, pre, load_sem.at[4])]
    for z in range(2):
        loads.append(
            pltpu.make_async_copy(down_window(z, 0), wd_cols.at[y, z], load_sem.at[5 + z])
        )
        for which, ref in enumerate((wg_hbm, wu_hbm)):
            loads.append(
                pltpu.make_async_copy(
                    wide_window(ref, z, 0), wide_at(z, which), load_sem.at[7 + 2 * z + which]
                )
            )
    for load in loads:
        load.start()

    for load in small:
        load.wait()
    lane2 = lax.broadcasted_iota(jnp.int32, (2, 128), 1)
    ids = ids_ref[...]
    local = lax.rem(ids, experts).astype(F32)
    row = (lax.div(ids, experts) * ROWS + slot_ref[...]).astype(F32)
    weight = weight_ref[...].astype(F32)
    meta = jnp.zeros((2, 128), F32)
    for k in range(8):
        for at, values in ((0, local), (8, row), (16, weight)):
            meta = jnp.where(lane2 == at + k, values[:, k : k + 1], meta)
    meta_high = pltpu.roll(meta, 64, 1)
    tokens = grad_ref[...].astype(F32)
    for b in range(SPLIT):
        cut = tokens[:, window(b) : window(b) + lanes]
        if b % 2 == 0:
            stage[b, :, 0:last] = cut[:, 0:last]
            stage[b, :, last:lanes] = jnp.where(lane2 < 64, cut[:, last:lanes], meta_high)
        else:
            stage[b, :, 0:128] = jnp.where(lane2 < 64, meta, cut[:, 0:128])
            stage[b, :, 128:lanes] = cut[:, 128:lanes]
    block_in[q] = stage[q]

    pl.semaphore_wait(barrier, len(partners))

    copies = []
    for d in range(1, SPLIT):
        target = lax.rem(q + d, SPLIT)
        copies.append(send(stage.at[target], block_in.at[q], a_sem, d - 1, in_block(target)))

    down_copies, wide_copies = [], []
    for step in (2, 1, 3):
        for z in range(2):
            down_copies.append(
                send(
                    down_window(z, step), wd_cols.at[y, z], wd_sem,
                    (step - 1) * 2 + z, along_y(step),
                )
            )
    for step in (2, 1, 3):
        for z in range(2):
            for which, ref in enumerate((wg_hbm, wu_hbm)):
                wide_copies.append(
                    send(
                        wide_window(ref, z, step), wide_at(z, which), wc_sem,
                        (step - 1) * 4 + z * 2 + which, along_y(step),
                    )
                )
    for copy in copies:
        copy.wait_recv()
    for b in range(SPLIT):
        block_rows[2 * b : 2 * b + 2, :] = block_in[b]
    xbuf[le] = block_rows[...].astype(BF16)

    def block(step):
        return lax.rem(le + step + experts, experts)

    def go(step, sems, index, target):
        return send(xbuf.at[block(step)], xbuf.at[block(step)], sems, index, target)

    lane_key = lax.broadcasted_iota(jnp.int32, (16, groups * ROWS), 1).astype(F32)
    my_local = le.astype(F32)

    def free_lanes(first, final):
        is_odd = jnp.full(first.shape, odd, jnp.int32) == 1
        return jnp.where(is_odd, first.astype(F32), pltpu.roll(final.astype(F32), 64, 1))

    def keys(found):
        return jnp.where(found == my_local, pltpu.roll(found, 120, 1), -1.0)

    def place(at):
        found = free_lanes(xbuf[at, :, 0:128], xbuf[at, :, last:lanes])
        key = keys(found)
        scale = pltpu.roll(found, 112, 1)
        ones = jnp.zeros(lane_key.shape, F32)
        scaled = jnp.zeros(lane_key.shape, F32)
        for k in range(8):
            hit = key[:, k : k + 1] == lane_key
            ones = jnp.where(hit, 1.0, ones)
            scaled = jnp.where(hit, scale[:, k : k + 1], scaled)
        pbuf[at] = ones.astype(BF16)
        wbuf[at] = scaled.astype(BF16)

    to_right = go(0, ar_sem, 0, right)
    to_left = go(0, al_sem, 0, left) if half > 1 else None
    near_right = go(0, anr_sem, 0, next_right)
    near_left = go(0, anl_sem, 0, next_left)
    place(le)
    for k in range(1, half + 1):
        last_right, last_left = near_right, near_left
        if k < half:
            to_left.wait_recv()
            if k < half - 1:
                to_left = go(2 * k, al_sem, k, left)
            near_left = go(2 * k, anl_sem, k, next_left)
        to_right.wait_recv()
        if k < half:
            to_right = go(-2 * k, ar_sem, k, right)
            near_right = go(-2 * k, anr_sem, k, next_right)
            place(block(2 * k))
        last_right.wait_recv()
        last_left.wait_recv()
        for step in (1 - 2 * k, 2 * k - 1, -2 * k):
            place(block(step))
    rows = lax.dot_general(
        pbuf[...].reshape(experts * 16, groups * ROWS),
        xbuf[...].reshape(experts * 16, lanes),
        TN, preferred_element_type=F32,
    )
    rbuf[...] = rows.astype(BF16).reshape(rbuf.shape)

    copies = []
    for d in range(1, groups):
        target = lax.rem(my_group + d, groups)
        for far, z in enumerate((zp, 1 - zp)):
            copies.append(
                send(
                    rbuf.at[target], ybuf.at[zp, my_group], b_sem, d * 2 + far, in_group(d, z)
                )
            )
    copies.append(send(rbuf.at[my_group], ybuf.at[zp, my_group], b_sem, 1, in_group(0, 1 - zp)))
    ybuf[zp, my_group] = rbuf[my_group]
    for copy in copies:
        copy.wait_recv()
    lane_row = lax.broadcasted_iota(jnp.int32, (slots, lanes), 1)
    kept = jnp.logical_and(lane_row >= 64 * odd, lane_row < part + 64 * odd)
    for z in range(2):
        dense = [ybuf[z, s].astype(F32)[0:cap] for s in range(groups)]
        dbuf[z] = jnp.where(kept, jnp.concatenate(dense, axis=0), 0.0).astype(BF16)

    size = slots // CHUNKS

    def rows_of(c):
        return pl.ds(c * size, size)

    for load in loads:
        load.wait()
    for copy in down_copies:
        copy.wait_recv()
    back_copies = []
    for c in range(CHUNKS):
        copies = []
        for step in (2, 1, 3, 0):
            at = lax.rem(y + step, 4)
            value = lax.dot_general(
                dbuf[0, rows_of(c), :], wd_cols[at, 0], NT, preferred_element_type=F32
            ) + lax.dot_general(
                dbuf[1, rows_of(c), :], wd_cols[at, 1], NT, preferred_element_type=F32
            )
            if step == 0:
                back[rows_of(c), :] = value
                continue
            bsend[step, rows_of(c), :] = value.astype(BF16)
            copies.append(
                send(
                    bsend.at[step, rows_of(c)], brecv.at[step, rows_of(c)], c_sem,
                    c * 4 + step, along_y(step),
                )
            )
        back_copies.append(copies)

    wide = []
    for c in range(CHUNKS):
        for copy in back_copies[c]:
            copy.wait_recv()
        rows = rows_of(c)
        proj = back[rows, :]
        for step in range(1, 4):
            proj = proj + brecv[step, rows, :].astype(F32)
        pre_gate = pre[0, rows, :].astype(F32)
        pre_up = pre[1, rows, :].astype(F32)
        sig = jax.nn.sigmoid(pre_gate)
        swish = pre_gate * sig
        gall[y, rows, 0:128] = (
            proj * pre_up * sig * (1.0 + pre_gate * (1.0 - sig))
        ).astype(BF16)
        gall[y, rows, 128:256] = (proj * swish).astype(BF16)
        copies = []
        for step in (2, 1, 3):
            copies.append(
                send(
                    gall.at[y, rows], gall.at[y, rows], d_sem, c * 4 + step, along_y(step)
                )
            )
        wide.append(copies)
        gate[rows, :] = jnp.broadcast_to(
            jnp.sum(swish * pre_up * proj, axis=1, keepdims=True), (size, 128)
        )
    for copy in wide_copies:
        copy.wait_recv()

    def to_group(z, s, sender_z, sender):
        return pltpu.make_async_remote_copy(
            src_ref=fbuf.at[z, s], dst_ref=vbuf.at[sender_z, sender],
            send_sem=f_sem.at[0, z * groups + s],
            recv_sem=f_sem.at[1, sender_z * groups + sender],
            device_id=(s, le * SPLIT + z * 4 + y), device_id_type=MESH,
        )

    def is_here(z, s):
        return jnp.logical_and(my_group == s, zp == z)

    blank = jnp.zeros((ROWS - cap, lanes), F32)
    lane_tile = lax.broadcasted_iota(jnp.int32, (size, 128), 1)
    free_first = jnp.logical_and(lane_tile < 64 * odd, lane_tile < 64)
    free_last = lane_tile >= 64 + 64 * odd
    for c in range(CHUNKS):
        for copy in wide[c]:
            copy.wait_recv()
        rows = rows_of(c)
        for z in range(2):
            value = lax.dot_general(gall[0, rows, :], wc[0, z], NT, preferred_element_type=F32)
            for at in range(1, 4):
                value = value + lax.dot_general(
                    gall[at, rows, :], wc[at, z], NT, preferred_element_type=F32
                )
            terms = gate[rows, :]
            value = jnp.concatenate(
                [
                    jnp.where(free_first, terms, value[:, 0:128]),
                    value[:, 128:last],
                    jnp.where(free_last, terms, value[:, last:lanes]),
                ],
                axis=1,
            )
            for at in range(size // cap):
                s = c * (size // cap) + at
                fbuf[z, s] = jnp.concatenate(
                    [value[at * cap : (at + 1) * cap], blank], axis=0
                ).astype(BF16)

                @pl.when(jnp.logical_not(is_here(z, s)))
                def _():
                    to_group(z, s, zp, my_group).start()

                @pl.when(is_here(z, s))
                def _():
                    vbuf[z, s] = fbuf[z, s]

    for z in range(2):
        for s in range(groups):

            @pl.when(jnp.logical_not(is_here(z, s)))
            def _():
                arriving = to_group(z, s, z, s)
                arriving.wait_recv()
                arriving.wait_send()

    count = experts * 16
    placed = pbuf[...].reshape(count, groups * ROWS)
    scaled = wbuf[...].reshape(count, groups * ROWS)
    row_group = lax.div(lax.broadcasted_iota(jnp.int32, (groups * ROWS, 128), 0), ROWS)
    lane_group = lax.broadcasted_iota(jnp.int32, (groups * ROWS, 128), 1)
    summed, terms = None, None
    for z in range(2):
        arrived = vbuf[z].reshape(groups * ROWS, lanes)
        spread = jnp.where(
            row_group == lane_group,
            free_lanes(arrived[:, 0:128], arrived[:, last:lanes]), 0.0,
        ).astype(BF16)
        more = lax.dot_general(scaled, arrived, NN, preferred_element_type=F32)
        more_terms = lax.dot_general(placed, spread, NN, preferred_element_type=F32)
        summed = more if summed is None else summed + more
        terms = more_terms if terms is None else terms + more_terms
    tokens_in = xbuf[...].reshape(count, lanes)
    key = keys(free_lanes(tokens_in[:, 0:128], tokens_in[:, last:lanes]))
    of_group = jnp.floor(key * (1.0 / ROWS))
    routed = jnp.zeros(key.shape, F32)
    for g in range(groups):
        routed = jnp.where(of_group == g, terms[:, g : g + 1], routed)
    lane_all = lax.broadcasted_iota(jnp.int32, key.shape, 1)
    ubuf[:, :, 0:128] = jnp.where(lane_all < 64 * odd, routed, summed[:, 0:128]).reshape(
        experts, 16, 128
    )
    ubuf[:, :, 128:last] = summed[:, 128:last].reshape(experts, 16, last - 128)
    ubuf[:, :, last:lanes] = jnp.where(
        lane_all >= 64 + 64 * odd, pltpu.roll(routed, 64, 1), summed[:, last:lanes]
    ).reshape(experts, 16, 128)

    ubf[...] = ubuf[...].astype(BF16)
    to_right = send(ubf.at[block(2 * half)], grr.at[0], gr_sem, 0, right)
    to_left = None
    near_right, near_left = [None] * half, [None] * half
    for k in range(half - 1, -1, -1):
        near_left[k] = send(ubf.at[block(-1 - 2 * k)], gnl.at[k], gnl_sem, k, next_left)
        near_right[k] = send(ubf.at[block(1 + 2 * k)], gnr.at[k], gnr_sem, k, next_right)
    for k in range(half - 1, 0, -1):
        at = half - 1 - k
        value = ubuf[block(-2 * k)]
        near_left[k].wait_recv()
        value = value + gnl[k].astype(F32)
        if to_left is not None:
            to_left.wait_recv()
            value = value + grl[at - 1].astype(F32)
        gsl[at] = value.astype(BF16)
        to_left = send(gsl.at[at], grl.at[at], gl_sem, at, left)
        value = ubuf[block(2 * k)]
        near_right[k].wait_recv()
        value = value + gnr[k].astype(F32)
        to_right.wait_recv()
        value = value + grr[at].astype(F32)
        gsr[at] = value.astype(BF16)
        to_right = send(gsr.at[at], grr.at[at + 1], gr_sem, at + 1, right)
    near_right[0].wait_recv()
    near_left[0].wait_recv()
    value = ubuf[le] + gnr[0].astype(F32) + gnl[0].astype(F32)
    if to_left is not None:
        to_left.wait_recv()
        value = value + grl[half - 2].astype(F32)
    to_right.wait_recv()
    value = value + grr[half - 1].astype(F32)

    block_rows[...] = value
    for b in range(SPLIT):
        fin[b] = block_rows[2 * b : 2 * b + 2, :]
    hbuf[q] = fin[q]
    copies = []
    for d in range(1, SPLIT):
        target = lax.rem(q + d, SPLIT)
        copies.append(send(fin.at[target], hbuf.at[q], h_sem, d - 1, in_block(target)))
    for copy in copies:
        copy.wait_recv()
    for m in range(SPLIT // 2):
        even, uneven = hbuf[2 * m], hbuf[2 * m + 1]
        base = 2 * part * m
        out_ref[:, base : base + last] = even[:, 0:last].astype(BF16)
        out_ref[:, base + last : base + lanes] = jnp.where(
            lane2 < 64, even[:, last:lanes], uneven[:, 0:128]
        ).astype(BF16)
        out_ref[:, base + lanes : base + 2 * part] = uneven[:, 128:lanes].astype(BF16)
    routing = pltpu.roll(hbuf[0][:, last:lanes] + hbuf[2][:, last:lanes], 64, 1)
    routing = routing + hbuf[1][:, 0:128] + hbuf[3][:, 0:128]
    routing_ref[...] = routing[:, 0:8]
    for copy in started:
        copy.wait_send()


def on_device(out_grad, routing_weight, expert_ids, slot_index, w_gate, w_up, w_down, pre_act):
    groups = lax.axis_size("group")
    experts = lax.axis_size("inner") // SPLIT
    cap = pre_act.shape[1] // groups
    width = out_grad.shape[1]
    lanes = -(-(width // SPLIT) // 128) * 128
    slots = groups * cap
    hidden = w_down.shape[0]
    half = experts // 4
    vmem = pltpu.VMEM
    dma = pltpu.SemaphoreType.DMA
    scratch = [
        vmem(out_grad.shape, BF16),
        vmem(routing_weight.shape, BF16),
        vmem(expert_ids.shape, jnp.int32),
        vmem(slot_index.shape, jnp.int32),
        vmem((4, 2, hidden, lanes), BF16),
        vmem((4, 2, lanes, 256), BF16),
        vmem((2, slots, hidden), BF16),
        vmem((SPLIT, 2, lanes), F32),
        vmem((SPLIT, 2, lanes), F32),
        vmem((16, lanes), F32),
        vmem((experts, 16, lanes), BF16),
        vmem((experts, 16, groups * ROWS), BF16),
        vmem((experts, 16, groups * ROWS), BF16),
        vmem((groups, ROWS, lanes), BF16),
        vmem((2, groups, ROWS, lanes), BF16),
        vmem((2, slots, lanes), BF16),
        vmem((4, slots, hidden), BF16),
        vmem((4, slots, hidden), BF16),
        vmem((slots, hidden), F32),
        vmem((4, slots, 256), BF16),
        vmem((slots, 128), F32),
        vmem((2, groups, ROWS, lanes), BF16),
        vmem((2, groups, ROWS, lanes), BF16),
        vmem((experts, 16, lanes), F32),
        vmem((experts, 16, lanes), BF16),
        vmem((half, 16, lanes), BF16),
        vmem((half, 16, lanes), BF16),
        vmem((half, 16, lanes), BF16),
        vmem((half, 16, lanes), BF16),
        vmem((half, 16, lanes), BF16),
        vmem((half, 16, lanes), BF16),
        vmem((SPLIT, 2, lanes), F32),
        vmem((SPLIT, 2, lanes), F32),
        dma((11,)),
        dma((2, SPLIT)),
        dma((2, half)),
        dma((2, half)),
        dma((2, half)),
        dma((2, half)),
        dma((2, 6)),
        dma((2, 12)),
        dma((2, 2 * groups)),
        dma((2, 4 * CHUNKS)),
        dma((2, 4 * CHUNKS)),
        dma((2, 2 * groups)),
        dma((2, half)),
        dma((2, half)),
        dma((2, half)),
        dma((2, half)),
        dma((2, SPLIT)),
    ]
    in_vmem = pl.BlockSpec(memory_space=pltpu.VMEM)
    anywhere = pl.BlockSpec(memory_space=pl.ANY)
    return pl.pallas_call(
        functools.partial(kernel, groups, experts, cap),
        out_shape=(
            jax.ShapeDtypeStruct(out_grad.shape, BF16),
            jax.ShapeDtypeStruct(expert_ids.shape, F32),
        ),
        in_specs=[anywhere] * 8,
        out_specs=(in_vmem, in_vmem),
        scratch_shapes=scratch,
        compiler_params=pltpu.CompilerParams(
            collective_id=0, has_side_effects=True, vmem_limit_bytes=60 * 2**20
        ),
        name="routed_backward",
    )(out_grad, routing_weight, expert_ids, slot_index, w_gate, w_up, w_down, pre_act)


def solution(mesh):
    token = P(("group", "inner"), None)
    in_specs = (
        token, token, token, token,
        P(None, ("group", "inner")),
        P(None, ("group", "inner")),
        P(("group", "inner"), None),
        P(None, None, ("group", "inner")),
    )
    return jax.shard_map(
        on_device, mesh=mesh, in_specs=in_specs, out_specs=(token, token), check_vma=False
    )
```

```python
import functools
import jax
import jax.numpy as jnp
from jax import lax
from jax.experimental import pallas as pl
from jax.experimental.pallas import tpu as pltpu
from jax.sharding import PartitionSpec as P

MESH = pl.DeviceIdType.MESH
F32 = jnp.float32
BF16 = jnp.bfloat16
SPLIT = 8
CHUNKS = 2
NT = (((1,), (1,)), ((), ()))
TN = (((0,), (0,)), ((), ()))
NN = (((1,), (0,)), ((), ()))


def kernel(
    groups, experts, cap,
    grad_hbm, weight_hbm, ids_hbm, slot_hbm, wg_hbm, wu_hbm, wd_hbm, pre_hbm,
    out_ref, routing_ref,
    grad_ref, weight_ref, ids_ref, slot_ref, wd_cols, wc, pre, stage, block_in,
    block_rows, xbuf, pbuf, wbuf, rbuf, ybuf, dbuf, bsend, brecv, back, gall, gate,
    fbuf, vbuf, ubuf, ubf, gr_out, gr_in, gn_in, fin, hbuf,
    load_sem, a_sem, ar_sem, an_sem, wd_sem, wc_sem, b_sem, c_sem, d_sem, f_sem,
    gr_sem, gn_sem, h_sem,
):
    my_group = lax.axis_index("group")
    my_inner = lax.axis_index("inner")
    le = lax.div(my_inner, SPLIT)
    q = lax.rem(my_inner, SPLIT)
    zp = lax.div(q, 4)
    y = lax.rem(q, 4)
    odd = lax.rem(y, 2)
    width = grad_ref.shape[1]
    part = width // SPLIT
    lanes = xbuf.shape[2]
    last = lanes - 128
    slots = groups * cap

    def window(index):
        return 2 * part * (index // 2) + last * (index % 2)

    def window_at(index):
        return 2 * part * lax.div(index, 2) + last * lax.rem(index, 2)

    def in_block(index):
        return (my_group, le * SPLIT + index)

    def in_ring(step):
        return (my_group, lax.rem(le + step + 2 * experts, experts) * SPLIT + q)

    def along_y(step):
        return in_block(zp * 4 + lax.rem(y + step, 4))

    def in_group(step, z):
        return (lax.rem(my_group + step, groups), le * SPLIT + z * 4 + y)

    routes = {
        0: [(1, 0), (-1, 0)],
        -3: [(1, -3), (-1, -3)],
        3: [(-1, 3), (1, 3)],
        -6: [(2, -6), (1, -6), (-1, -6)],
        6: [(-1, 6), (1, 6)],
    }
    aside = [route for of in (0, -3, 3, -6, 6) for route in routes[of]]
    right, left = in_ring(3), in_ring(-3)

    def send(src, dst, sems, index, target):
        copy = pltpu.make_async_remote_copy(
            src_ref=src, dst_ref=dst, send_sem=sems.at[0, index],
            recv_sem=sems.at[1, index], device_id=target, device_id_type=MESH,
        )
        copy.start()
        started.append(copy)
        return copy

    started = []
    small = [
        pltpu.make_async_copy(grad_hbm, grad_ref, load_sem.at[0]),
        pltpu.make_async_copy(weight_hbm, weight_ref, load_sem.at[1]),
        pltpu.make_async_copy(ids_hbm, ids_ref, load_sem.at[2]),
        pltpu.make_async_copy(slot_hbm, slot_ref, load_sem.at[3]),
    ]
    for load in small:
        load.start()

    barrier = pltpu.get_barrier_semaphore()
    partners = [in_block(lax.rem(q + d, SPLIT)) for d in range(1, SPLIT)]
    partners += [right, left] + [in_ring(step) for step in (1, -1, -2)]
    partners += [in_group(d, z) for d in range(1, groups) for z in (zp, 1 - zp)]
    for partner in partners:
        pl.semaphore_signal(barrier, inc=1, device_id=partner, device_id_type=MESH)

    def down_window(z, step):
        at = window_at(z * 4 + lax.rem(y + step, 4))
        return wd_hbm.at[:, pl.ds(pl.multiple_of(at, 128), lanes)]

    def wide_window(ref, z, step):
        index = z * 4 + lax.rem(y + step, 4)
        return ref.at[pl.ds(pl.multiple_of(part * index, 64), part), :]

    def wide_at(z, which, step):
        start = pl.multiple_of(64 * lax.rem(y + step, 2), 64)
        return wc.at[y, z, pl.ds(start, part), pl.ds(128 * which, 128)]

    loads = [pltpu.make_async_copy(pre_hbm, pre, load_sem.at[4])]
    for z in range(2):
        loads.append(
            pltpu.make_async_copy(down_window(z, 0), wd_cols.at[y, z], load_sem.at[5 + z])
        )
        for which, ref in enumerate((wg_hbm, wu_hbm)):
            loads.append(
                pltpu.make_async_copy(
                    wide_window(ref, z, 0), wide_at(z, which, 0), load_sem.at[7 + 2 * z + which]
                )
            )

    for load in small:
        load.wait()
    lane2 = lax.broadcasted_iota(jnp.int32, (2, 128), 1)
    ids = ids_ref[...]
    local = lax.rem(ids, experts).astype(F32)
    row = (lax.div(ids, experts) * cap + slot_ref[...]).astype(F32)
    weight = weight_ref[...].astype(F32)
    meta = jnp.zeros((2, 128), F32)
    for k in range(8):
        for at, values in ((0, local), (8, row), (16, weight)):
            meta = jnp.where(lane2 == at + k, values[:, k : k + 1], meta)
    meta_high = pltpu.roll(meta, 64, 1)
    tokens = grad_ref[...].astype(F32)
    for b in range(SPLIT):
        cut = tokens[:, window(b) : window(b) + lanes]
        if b % 2 == 0:
            stage[b, :, 0:last] = cut[:, 0:last]
            stage[b, :, last:lanes] = jnp.where(lane2 < 64, cut[:, last:lanes], meta_high)
        else:
            stage[b, :, 0:128] = jnp.where(lane2 < 64, meta, cut[:, 0:128])
            stage[b, :, 128:lanes] = cut[:, 128:lanes]
    block_in[q] = stage[q]

    pl.semaphore_wait(barrier, len(partners))

    copies = []
    for d in range(1, SPLIT):
        target = lax.rem(q + d, SPLIT)
        copies.append(send(stage.at[target], block_in.at[q], a_sem, d - 1, in_block(target)))

    down_copies, wide_copies = [], []

    def change_down():
        for step in (2, 1, 3):
            for z in range(2):
                down_copies.append(
                    send(
                        down_window(z, step), wd_cols.at[y, z], wd_sem,
                        (step - 1) * 2 + z, along_y(step),
                    )
                )

    def change_wide():
        for step in (2, 1, 3):
            for z in range(2):
                for which, ref in enumerate((wg_hbm, wu_hbm)):
                    wide_copies.append(
                        send(
                            wide_window(ref, z, step), wide_at(z, which, step), wc_sem,
                            (step - 1) * 4 + z * 2 + which, along_y(step),
                        )
                    )

    change_down()
    change_wide()
    for load in loads:
        load.start()
    for copy in copies:
        copy.wait_recv()
    for b in range(SPLIT):
        block_rows[2 * b : 2 * b + 2, :] = block_in[b]
    xbuf[le] = block_rows[...].astype(BF16)

    def block(step):
        return lax.rem(le + step + 2 * experts, experts)

    def go(step, sems, index, target):
        return send(xbuf.at[block(step)], xbuf.at[block(step)], sems, index, target)

    def go_aside(of):
        return [
            (go(of, an_sem, aside.index(route), in_ring(route[0])), of - route[0])
            for route in routes[of]
        ]

    def take(arriving):
        for copy, step in arriving:
            copy.wait_recv()
            place(block(step))

    lane_key = lax.broadcasted_iota(jnp.int32, (16, slots), 1).astype(F32)
    my_local = le.astype(F32)

    def free_lanes(first, final):
        is_odd = jnp.full(first.shape, odd, jnp.int32) == 1
        return jnp.where(is_odd, first.astype(F32), pltpu.roll(final.astype(F32), 64, 1))

    def keys(found):
        return jnp.where(found == my_local, pltpu.roll(found, 120, 1), -1.0)

    def place(at):
        found = free_lanes(xbuf[at, :, 0:128], xbuf[at, :, last:lanes])
        key = keys(found)
        scale = pltpu.roll(found, 112, 1)
        ones = jnp.zeros(lane_key.shape, F32)
        scaled = jnp.zeros(lane_key.shape, F32)
        for k in range(8):
            hit = key[:, k : k + 1] == lane_key
            ones = jnp.where(hit, 1.0, ones)
            scaled = jnp.where(hit, scale[:, k : k + 1], scaled)
        pbuf[at] = ones.astype(BF16)
        wbuf[at] = scaled.astype(BF16)

    right_1 = go(0, ar_sem, 0, right)
    left_1 = go(0, ar_sem, 1, left)
    arriving = go_aside(0)
    place(le)
    take(arriving)
    right_1.wait_recv()
    right_2 = go(-3, ar_sem, 2, right)
    arriving = go_aside(-3)
    left_1.wait_recv()
    left_2 = go(3, ar_sem, 3, left)
    arriving += go_aside(3)
    place(block(-3))
    place(block(3))
    take(arriving)
    right_2.wait_recv()
    arriving = go_aside(-6)
    left_2.wait_recv()
    arriving += go_aside(6)
    place(block(-6))
    place(block(6))
    take(arriving[1:] + arriving[:1])
    def fold(value):
        middle = lanes // 2
        return jnp.concatenate([value[:, 0:middle], value[:, middle:lanes]], axis=0).astype(BF16)

    def unfold(value):
        value = value.astype(F32)
        return jnp.concatenate([value[0:cap], value[cap : 2 * cap]], axis=1)

    rows = lax.dot_general(
        pbuf[...].reshape(experts * 16, slots),
        xbuf[...].reshape(experts * 16, lanes),
        TN, preferred_element_type=F32,
    )
    for g in range(groups):
        rbuf[g] = fold(rows[g * cap : (g + 1) * cap])

    copies = []
    for d in range(1, groups):
        target = lax.rem(my_group + d, groups)
        for far, z in enumerate((zp, 1 - zp)):
            copies.append(
                send(
                    rbuf.at[target], ybuf.at[zp, my_group], b_sem, d * 2 + far, in_group(d, z)
                )
            )
    copies.append(send(rbuf.at[my_group], ybuf.at[zp, my_group], b_sem, 1, in_group(0, 1 - zp)))
    ybuf[zp, my_group] = rbuf[my_group]
    for copy in copies:
        copy.wait_recv()
    lane_row = lax.broadcasted_iota(jnp.int32, (slots, lanes), 1)
    kept = jnp.logical_and(lane_row >= 64 * odd, lane_row < part + 64 * odd)
    for z in range(2):
        dense = [unfold(ybuf[z, s]) for s in range(groups)]
        dbuf[z] = jnp.where(kept, jnp.concatenate(dense, axis=0), 0.0).astype(BF16)

    size = slots // CHUNKS

    def rows_of(c):
        return pl.ds(c * size, size)

    for load in loads:
        load.wait()
    for copy in down_copies:
        copy.wait_recv()
    back_copies = []
    for c in range(CHUNKS):
        copies = []
        for step in (2, 1, 3, 0):
            at = lax.rem(y + step, 4)
            value = lax.dot_general(
                dbuf[0, rows_of(c), :], wd_cols[at, 0], NT, preferred_element_type=F32
            ) + lax.dot_general(
                dbuf[1, rows_of(c), :], wd_cols[at, 1], NT, preferred_element_type=F32
            )
            if step == 0:
                back[rows_of(c), :] = value
                continue
            bsend[step, rows_of(c), :] = value.astype(BF16)
            copies.append(
                send(
                    bsend.at[step, rows_of(c)], brecv.at[step, rows_of(c)], c_sem,
                    c * 4 + step, along_y(step),
                )
            )
        back_copies.append(copies)

    wide = []
    for c in range(CHUNKS):
        for copy in back_copies[c]:
            copy.wait_recv()
        rows = rows_of(c)
        proj = back[rows, :]
        for step in range(1, 4):
            proj = proj + brecv[step, rows, :].astype(F32)
        pre_gate = pre[0, rows, :].astype(F32)
        pre_up = pre[1, rows, :].astype(F32)
        sig = jax.nn.sigmoid(pre_gate)
        swish = pre_gate * sig
        gall[y, rows, 0:128] = (
            proj * pre_up * sig * (1.0 + pre_gate * (1.0 - sig))
        ).astype(BF16)
        gall[y, rows, 128:256] = (proj * swish).astype(BF16)
        copies = []
        for step in (2, 1, 3):
            copies.append(
                send(
                    gall.at[y, rows], gall.at[y, rows], d_sem, c * 4 + step, along_y(step)
                )
            )
        wide.append(copies)
        gate[rows, :] = jnp.broadcast_to(
            jnp.sum(swish * pre_up * proj, axis=1, keepdims=True), (size, 128)
        )
    for copy in wide_copies:
        copy.wait_recv()

    def to_group(z, s, sender_z, sender):
        return pltpu.make_async_remote_copy(
            src_ref=fbuf.at[z, s], dst_ref=vbuf.at[sender_z, sender],
            send_sem=f_sem.at[0, z * groups + s],
            recv_sem=f_sem.at[1, sender_z * groups + sender],
            device_id=(s, le * SPLIT + z * 4 + y), device_id_type=MESH,
        )

    def is_here(z, s):
        return jnp.logical_and(my_group == s, zp == z)

    lane_tile = lax.broadcasted_iota(jnp.int32, (size, 128), 1)
    free_first = jnp.logical_and(lane_tile < 64 * odd, lane_tile < 64)
    free_last = lane_tile >= 64 + 64 * odd
    for c in range(CHUNKS):
        for copy in wide[c]:
            copy.wait_recv()
        rows = rows_of(c)
        for z in range(2):
            value = lax.dot_general(gall[0, rows, :], wc[0, z], NT, preferred_element_type=F32)
            for at in range(1, 4):
                value = value + lax.dot_general(
                    gall[at, rows, :], wc[at, z], NT, preferred_element_type=F32
                )
            terms = gate[rows, :]
            value = jnp.concatenate(
                [
                    jnp.where(free_first, terms, value[:, 0:128]),
                    value[:, 128:last],
                    jnp.where(free_last, terms, value[:, last:lanes]),
                ],
                axis=1,
            )
            for at in range(size // cap):
                s = c * (size // cap) + at
                fbuf[z, s] = fold(value[at * cap : (at + 1) * cap])

                @pl.when(jnp.logical_not(is_here(z, s)))
                def _():
                    to_group(z, s, zp, my_group).start()

                @pl.when(is_here(z, s))
                def _():
                    vbuf[z, s] = fbuf[z, s]

    for z in range(2):
        for s in range(groups):

            @pl.when(jnp.logical_not(is_here(z, s)))
            def _():
                arriving = to_group(z, s, z, s)
                arriving.wait_recv()
                arriving.wait_send()

    count = experts * 16
    placed = pbuf[...].reshape(count, slots)
    scaled = wbuf[...].reshape(count, slots)
    row_group = lax.div(lax.broadcasted_iota(jnp.int32, (slots, 128), 0), cap)
    lane_group = lax.broadcasted_iota(jnp.int32, (slots, 128), 1)
    summed, terms = None, None
    for z in range(2):
        whole = jnp.concatenate([unfold(vbuf[z, g]) for g in range(groups)], axis=0)
        arrived = whole.astype(BF16)
        spread = jnp.where(
            row_group == lane_group,
            free_lanes(whole[:, 0:128], whole[:, last:lanes]), 0.0,
        ).astype(BF16)
        more = lax.dot_general(scaled, arrived, NN, preferred_element_type=F32)
        more_terms = lax.dot_general(placed, spread, NN, preferred_element_type=F32)
        summed = more if summed is None else summed + more
        terms = more_terms if terms is None else terms + more_terms
    tokens_in = xbuf[...].reshape(count, lanes)
    key = keys(free_lanes(tokens_in[:, 0:128], tokens_in[:, last:lanes]))
    of_group = jnp.floor((key + 0.5) * (1.0 / cap))
    routed = jnp.zeros(key.shape, F32)
    for g in range(groups):
        routed = jnp.where(of_group == g, terms[:, g : g + 1], routed)
    lane_all = lax.broadcasted_iota(jnp.int32, key.shape, 1)
    ubuf[:, :, 0:128] = jnp.where(lane_all < 64 * odd, routed, summed[:, 0:128]).reshape(
        experts, 16, 128
    )
    ubuf[:, :, 128:last] = summed[:, 128:last].reshape(experts, 16, last - 128)
    ubuf[:, :, last:lanes] = jnp.where(
        lane_all >= 64 + 64 * odd, pltpu.roll(routed, 64, 1), summed[:, last:lanes]
    ).reshape(experts, 16, 128)

    ubf[...] = ubuf[...].astype(BF16)
    nearer = {}
    for of in (-6, 6, -3, 3, 0):
        for route in routes[of]:
            at = aside.index(route)
            nearer[route] = send(
                ubf.at[block(of - route[0])], gn_in.at[at], gn_sem, at, in_ring(-route[0])
            )

    def with_aside(of):
        value = ubuf[block(of)]
        for route in routes[of]:
            nearer[route].wait_recv()
            value = value + gn_in[aside.index(route)].astype(F32)
        return value

    def go_back(value, index, target):
        gr_out[index] = value.astype(BF16)
        return send(gr_out.at[index], gr_in.at[index], gr_sem, index, target)

    right_2 = go_back(with_aside(6), 3, right)
    left_2 = go_back(with_aside(-6), 2, left)
    value = with_aside(3)
    right_2.wait_recv()
    right_1 = go_back(value + gr_in[3].astype(F32), 1, right)
    value = with_aside(-3)
    left_2.wait_recv()
    left_1 = go_back(value + gr_in[2].astype(F32), 0, left)
    value = with_aside(0)
    right_1.wait_recv()
    left_1.wait_recv()
    value = value + gr_in[0].astype(F32) + gr_in[1].astype(F32)

    block_rows[...] = value
    for b in range(SPLIT):
        fin[b] = block_rows[2 * b : 2 * b + 2, :]
    hbuf[q] = fin[q]
    copies = []
    for d in range(1, SPLIT):
        target = lax.rem(q + d, SPLIT)
        copies.append(send(fin.at[target], hbuf.at[q], h_sem, d - 1, in_block(target)))
    for copy in copies:
        copy.wait_recv()
    for m in range(SPLIT // 2):
        even, uneven = hbuf[2 * m], hbuf[2 * m + 1]
        base = 2 * part * m
        out_ref[:, base : base + last] = even[:, 0:last].astype(BF16)
        out_ref[:, base + last : base + lanes] = jnp.where(
            lane2 < 64, even[:, last:lanes], uneven[:, 0:128]
        ).astype(BF16)
        out_ref[:, base + lanes : base + 2 * part] = uneven[:, 128:lanes].astype(BF16)
    routing = pltpu.roll(hbuf[0][:, last:lanes] + hbuf[2][:, last:lanes], 64, 1)
    routing = routing + hbuf[1][:, 0:128] + hbuf[3][:, 0:128]
    routing_ref[...] = routing[:, 0:8]
    for copy in started:
        copy.wait_send()


def on_device(out_grad, routing_weight, expert_ids, slot_index, w_gate, w_up, w_down, pre_act):
    groups = lax.axis_size("group")
    experts = lax.axis_size("inner") // SPLIT
    cap = pre_act.shape[1] // groups
    width = out_grad.shape[1]
    lanes = -(-(width // SPLIT) // 128) * 128
    slots = groups * cap
    hidden = w_down.shape[0]
    vmem = pltpu.VMEM
    dma = pltpu.SemaphoreType.DMA
    scratch = [
        vmem(out_grad.shape, BF16),
        vmem(routing_weight.shape, BF16),
        vmem(expert_ids.shape, jnp.int32),
        vmem(slot_index.shape, jnp.int32),
        vmem((4, 2, hidden, lanes), BF16),
        vmem((4, 2, lanes, 256), BF16),
        vmem((2, slots, hidden), BF16),
        vmem((SPLIT, 2, lanes), F32),
        vmem((SPLIT, 2, lanes), F32),
        vmem((16, lanes), F32),
        vmem((experts, 16, lanes), BF16),
        vmem((experts, 16, slots), BF16),
        vmem((experts, 16, slots), BF16),
        vmem((groups, 2 * cap, lanes // 2), BF16),
        vmem((2, groups, 2 * cap, lanes // 2), BF16),
        vmem((2, slots, lanes), BF16),
        vmem((4, slots, hidden), BF16),
        vmem((4, slots, hidden), BF16),
        vmem((slots, hidden), F32),
        vmem((4, slots, 256), BF16),
        vmem((slots, 128), F32),
        vmem((2, groups, 2 * cap, lanes // 2), BF16),
        vmem((2, groups, 2 * cap, lanes // 2), BF16),
        vmem((experts, 16, lanes), F32),
        vmem((experts, 16, lanes), BF16),
        vmem((4, 16, lanes), BF16),
        vmem((4, 16, lanes), BF16),
        vmem((11, 16, lanes), BF16),
        vmem((SPLIT, 2, lanes), F32),
        vmem((SPLIT, 2, lanes), F32),
        dma((11,)),
        dma((2, SPLIT)),
        dma((2, 4)),
        dma((2, 11)),
        dma((2, 6)),
        dma((2, 12)),
        dma((2, 2 * groups)),
        dma((2, 4 * CHUNKS)),
        dma((2, 4 * CHUNKS)),
        dma((2, 2 * groups)),
        dma((2, 4)),
        dma((2, 11)),
        dma((2, SPLIT)),
    ]
    in_vmem = pl.BlockSpec(memory_space=pltpu.VMEM)
    anywhere = pl.BlockSpec(memory_space=pl.ANY)
    return pl.pallas_call(
        functools.partial(kernel, groups, experts, cap),
        out_shape=(
            jax.ShapeDtypeStruct(out_grad.shape, BF16),
            jax.ShapeDtypeStruct(expert_ids.shape, F32),
        ),
        in_specs=[anywhere] * 8,
        out_specs=(in_vmem, in_vmem),
        scratch_shapes=scratch,
        compiler_params=pltpu.CompilerParams(
            collective_id=0, has_side_effects=True, vmem_limit_bytes=60 * 2**20
        ),
        name="routed_backward",
    )(out_grad, routing_weight, expert_ids, slot_index, w_gate, w_up, w_down, pre_act)


def solution(mesh):
    token = P(("group", "inner"), None)
    in_specs = (
        token, token, token, token,
        P(None, ("group", "inner")),
        P(None, ("group", "inner")),
        P(("group", "inner"), None),
        P(None, None, ("group", "inner")),
    )
    return jax.shard_map(
        on_device, mesh=mesh, in_specs=in_specs, out_specs=(token, token), check_vma=False
    )
```

```python
import functools
import jax
import jax.numpy as jnp
from jax import lax
from jax.experimental import pallas as pl
from jax.experimental.pallas import tpu as pltpu
from jax.sharding import PartitionSpec as P

MESH = pl.DeviceIdType.MESH
F32 = jnp.float32
BF16 = jnp.bfloat16
SPLIT = 8
CHUNKS = 4
NT = (((1,), (1,)), ((), ()))
TN = (((0,), (0,)), ((), ()))
NN = (((1,), (0,)), ((), ()))


def kernel(
    groups, experts, cap,
    grad_hbm, weight_hbm, ids_hbm, slot_hbm, wg_hbm, wu_hbm, wd_hbm, pre_hbm,
    out_ref, routing_ref,
    grad_ref, weight_ref, ids_ref, slot_ref, wd_cols, wc, pre, stage, block_in,
    block_rows, xbuf, pbuf, wbuf, rbuf, ybuf, dbuf, bsend, brecv, back, gall, gate,
    fbuf, vbuf, ubuf, ubf, gr_out, gr_in, gn_in, fin, hbuf,
    load_sem, a_sem, ar_sem, an_sem, wd_sem, wc_sem, b_sem, c_sem, d_sem, f_sem,
    gr_sem, gn_sem, h_sem,
):
    my_group = lax.axis_index("group")
    my_inner = lax.axis_index("inner")
    le = lax.div(my_inner, SPLIT)
    q = lax.rem(my_inner, SPLIT)
    zp = lax.div(q, 4)
    y = lax.rem(q, 4)
    odd = lax.rem(y, 2)
    width = grad_ref.shape[1]
    part = width // SPLIT
    lanes = xbuf.shape[2]
    last = lanes - 128
    slots = groups * cap

    def window(index):
        return 2 * part * (index // 2) + last * (index % 2)

    def window_at(index):
        return 2 * part * lax.div(index, 2) + last * lax.rem(index, 2)

    def in_block(index):
        return (my_group, le * SPLIT + index)

    def in_ring(step):
        return (my_group, lax.rem(le + step + 2 * experts, experts) * SPLIT + q)

    def along_y(step):
        return in_block(zp * 4 + lax.rem(y + step, 4))

    def in_group(step, z):
        return (lax.rem(my_group + step, groups), le * SPLIT + z * 4 + y)

    routes = {
        0: [(1, 0), (-1, 0)],
        -3: [(1, -3), (-1, -3)],
        3: [(-1, 3), (1, 3)],
        -6: [(2, -6), (1, -6), (-1, -6)],
        6: [(-1, 6), (1, 6)],
    }
    aside = [route for of in (0, -3, 3, -6, 6) for route in routes[of]]
    right, left = in_ring(3), in_ring(-3)

    def send(src, dst, sems, index, target):
        copy = pltpu.make_async_remote_copy(
            src_ref=src, dst_ref=dst, send_sem=sems.at[0, index],
            recv_sem=sems.at[1, index], device_id=target, device_id_type=MESH,
        )
        copy.start()
        started.append(copy)
        return copy

    started = []
    small = [
        pltpu.make_async_copy(grad_hbm, grad_ref, load_sem.at[0]),
        pltpu.make_async_copy(weight_hbm, weight_ref, load_sem.at[1]),
        pltpu.make_async_copy(ids_hbm, ids_ref, load_sem.at[2]),
        pltpu.make_async_copy(slot_hbm, slot_ref, load_sem.at[3]),
    ]
    for load in small:
        load.start()

    barrier = pltpu.get_barrier_semaphore()
    partners = [in_block(lax.rem(q + d, SPLIT)) for d in range(1, SPLIT)]
    partners += [right, left] + [in_ring(step) for step in (1, -1, -2)]
    partners += [in_group(d, z) for d in range(1, groups) for z in (zp, 1 - zp)]
    for partner in partners:
        pl.semaphore_signal(barrier, inc=1, device_id=partner, device_id_type=MESH)

    def down_window(z, step):
        at = window_at(z * 4 + lax.rem(y + step, 4))
        return wd_hbm.at[:, pl.ds(pl.multiple_of(at, 128), lanes)]

    def wide_window(ref, z, step):
        index = z * 4 + lax.rem(y + step, 4)
        return ref.at[pl.ds(pl.multiple_of(part * index, 64), part), :]

    def wide_at(z, which, step):
        start = pl.multiple_of(64 * lax.rem(y + step, 2), 64)
        return wc.at[y, z, pl.ds(start, part), pl.ds(128 * which, 128)]

    loads = [pltpu.make_async_copy(pre_hbm, pre, load_sem.at[4])]
    for z in range(2):
        loads.append(
            pltpu.make_async_copy(down_window(z, 0), wd_cols.at[y, z], load_sem.at[5 + z])
        )
        for which, ref in enumerate((wg_hbm, wu_hbm)):
            loads.append(
                pltpu.make_async_copy(
                    wide_window(ref, z, 0), wide_at(z, which, 0), load_sem.at[7 + 2 * z + which]
                )
            )

    for load in small:
        load.wait()
    lane2 = lax.broadcasted_iota(jnp.int32, (2, 128), 1)
    ids = ids_ref[...]
    local = lax.rem(ids, experts).astype(F32)
    row = (lax.div(ids, experts) * cap + slot_ref[...]).astype(F32)
    weight = weight_ref[...].astype(F32)
    meta = jnp.zeros((2, 128), F32)
    for k in range(8):
        for at, values in ((0, local), (8, row), (16, weight)):
            meta = jnp.where(lane2 == at + k, values[:, k : k + 1], meta)
    meta_high = pltpu.roll(meta, 64, 1)
    tokens = grad_ref[...].astype(F32)
    for b in range(SPLIT):
        cut = tokens[:, window(b) : window(b) + lanes]
        if b % 2 == 0:
            stage[b, :, 0:last] = cut[:, 0:last]
            stage[b, :, last:lanes] = jnp.where(lane2 < 64, cut[:, last:lanes], meta_high)
        else:
            stage[b, :, 0:128] = jnp.where(lane2 < 64, meta, cut[:, 0:128])
            stage[b, :, 128:lanes] = cut[:, 128:lanes]
    block_in[q] = stage[q]

    pl.semaphore_wait(barrier, len(partners))

    copies = []
    for d in range(1, SPLIT):
        target = lax.rem(q + d, SPLIT)
        copies.append(send(stage.at[target], block_in.at[q], a_sem, d - 1, in_block(target)))

    down_copies, wide_copies = [], []

    def change_down():
        for step in (2, 1, 3):
            for z in range(2):
                down_copies.append(
                    send(
                        down_window(z, step), wd_cols.at[y, z], wd_sem,
                        (step - 1) * 2 + z, along_y(step),
                    )
                )

    def change_wide():
        for step in (2, 1, 3):
            for z in range(2):
                for which, ref in enumerate((wg_hbm, wu_hbm)):
                    wide_copies.append(
                        send(
                            wide_window(ref, z, step), wide_at(z, which, step), wc_sem,
                            (step - 1) * 4 + z * 2 + which, along_y(step),
                        )
                    )

    change_down()
    change_wide()
    for load in loads:
        load.start()
    for copy in copies:
        copy.wait_recv()
    for b in range(SPLIT):
        block_rows[2 * b : 2 * b + 2, :] = block_in[b]
    xbuf[le] = block_rows[...].astype(BF16)

    def block(step):
        return lax.rem(le + step + 2 * experts, experts)

    def go(step, sems, index, target):
        return send(xbuf.at[block(step)], xbuf.at[block(step)], sems, index, target)

    def go_aside(of):
        return [
            (go(of, an_sem, aside.index(route), in_ring(route[0])), of - route[0])
            for route in routes[of]
        ]

    def take(arriving):
        for copy, step in arriving:
            copy.wait_recv()
            place(block(step))

    lane_key = lax.broadcasted_iota(jnp.int32, (16, slots), 1).astype(F32)
    my_local = le.astype(F32)

    def free_lanes(first, final):
        is_odd = jnp.full(first.shape, odd, jnp.int32) == 1
        return jnp.where(is_odd, first.astype(F32), pltpu.roll(final.astype(F32), 64, 1))

    def keys(found):
        return jnp.where(found == my_local, pltpu.roll(found, 120, 1), -1.0)

    def place(at):
        found = free_lanes(xbuf[at, :, 0:128], xbuf[at, :, last:lanes])
        key = keys(found)
        scale = pltpu.roll(found, 112, 1)
        ones = jnp.zeros(lane_key.shape, F32)
        scaled = jnp.zeros(lane_key.shape, F32)
        for k in range(8):
            hit = key[:, k : k + 1] == lane_key
            ones = jnp.where(hit, 1.0, ones)
            scaled = jnp.where(hit, scale[:, k : k + 1], scaled)
        pbuf[at] = ones.astype(BF16)
        wbuf[at] = scaled.astype(BF16)

    right_1 = go(0, ar_sem, 0, right)
    left_1 = go(0, ar_sem, 1, left)
    arriving = go_aside(0)
    place(le)
    take(arriving)
    right_1.wait_recv()
    right_2 = go(-3, ar_sem, 2, right)
    arriving = go_aside(-3)
    left_1.wait_recv()
    left_2 = go(3, ar_sem, 3, left)
    arriving += go_aside(3)
    place(block(-3))
    place(block(3))
    take(arriving)
    right_2.wait_recv()
    arriving = go_aside(-6)
    left_2.wait_recv()
    arriving += go_aside(6)
    place(block(-6))
    place(block(6))
    take(arriving[1:] + arriving[:1])
    def fold(value):
        middle = lanes // 2
        return jnp.concatenate([value[:, 0:middle], value[:, middle:lanes]], axis=0).astype(BF16)

    def unfold(value):
        value = value.astype(F32)
        return jnp.concatenate([value[0:cap], value[cap : 2 * cap]], axis=1)

    rows = lax.dot_general(
        pbuf[...].reshape(experts * 16, slots),
        xbuf[...].reshape(experts * 16, lanes),
        TN, preferred_element_type=F32,
    )
    for g in range(groups):
        rbuf[g] = fold(rows[g * cap : (g + 1) * cap])

    copies = []
    for d in range(1, groups):
        target = lax.rem(my_group + d, groups)
        for far, z in enumerate((zp, 1 - zp)):
            copies.append(
                send(
                    rbuf.at[target], ybuf.at[zp, my_group], b_sem, d * 2 + far, in_group(d, z)
                )
            )
    copies.append(send(rbuf.at[my_group], ybuf.at[zp, my_group], b_sem, 1, in_group(0, 1 - zp)))
    ybuf[zp, my_group] = rbuf[my_group]
    for copy in copies:
        copy.wait_recv()
    lane_row = lax.broadcasted_iota(jnp.int32, (slots, lanes), 1)
    kept = jnp.logical_and(lane_row >= 64 * odd, lane_row < part + 64 * odd)
    for z in range(2):
        dense = [unfold(ybuf[z, s]) for s in range(groups)]
        dbuf[z] = jnp.where(kept, jnp.concatenate(dense, axis=0), 0.0).astype(BF16)

    size = slots // CHUNKS

    def rows_of(c):
        return pl.ds(c * size, size)

    for load in loads:
        load.wait()
    for copy in down_copies:
        copy.wait_recv()
    back_copies = []
    for c in range(CHUNKS):
        copies = []
        for step in (2, 1, 3, 0):
            at = lax.rem(y + step, 4)
            value = lax.dot_general(
                dbuf[0, rows_of(c), :], wd_cols[at, 0], NT, preferred_element_type=F32
            ) + lax.dot_general(
                dbuf[1, rows_of(c), :], wd_cols[at, 1], NT, preferred_element_type=F32
            )
            if step == 0:
                back[rows_of(c), :] = value
                continue
            bsend[step, rows_of(c), :] = value.astype(BF16)
            copies.append(
                send(
                    bsend.at[step, rows_of(c)], brecv.at[step, rows_of(c)], c_sem,
                    c * 4 + step, along_y(step),
                )
            )
        back_copies.append(copies)

    wide = []
    for c in range(CHUNKS):
        for copy in back_copies[c]:
            copy.wait_recv()
        rows = rows_of(c)
        proj = back[rows, :]
        for step in range(1, 4):
            proj = proj + brecv[step, rows, :].astype(F32)
        pre_gate = pre[0, rows, :].astype(F32)
        pre_up = pre[1, rows, :].astype(F32)
        sig = jax.nn.sigmoid(pre_gate)
        swish = pre_gate * sig
        gall[y, rows, 0:128] = (
            proj * pre_up * sig * (1.0 + pre_gate * (1.0 - sig))
        ).astype(BF16)
        gall[y, rows, 128:256] = (proj * swish).astype(BF16)
        copies = []
        for step in (2, 1, 3):
            copies.append(
                send(
                    gall.at[y, rows], gall.at[y, rows], d_sem, c * 4 + step, along_y(step)
                )
            )
        wide.append(copies)
        gate[rows, :] = jnp.broadcast_to(
            jnp.sum(swish * pre_up * proj, axis=1, keepdims=True), (size, 128)
        )
    for copy in wide_copies:
        copy.wait_recv()

    def to_group(z, s, sender_z, sender):
        return pltpu.make_async_remote_copy(
            src_ref=fbuf.at[z, s], dst_ref=vbuf.at[sender_z, sender],
            send_sem=f_sem.at[0, z * groups + s],
            recv_sem=f_sem.at[1, sender_z * groups + sender],
            device_id=(s, le * SPLIT + z * 4 + y), device_id_type=MESH,
        )

    def is_here(z, s):
        return jnp.logical_and(my_group == s, zp == z)

    lane_tile = lax.broadcasted_iota(jnp.int32, (size, 128), 1)
    free_first = jnp.logical_and(lane_tile < 64 * odd, lane_tile < 64)
    free_last = lane_tile >= 64 + 64 * odd
    for c in range(CHUNKS):
        for copy in wide[c]:
            copy.wait_recv()
        rows = rows_of(c)
        for z in range(2):
            value = lax.dot_general(gall[0, rows, :], wc[0, z], NT, preferred_element_type=F32)
            for at in range(1, 4):
                value = value + lax.dot_general(
                    gall[at, rows, :], wc[at, z], NT, preferred_element_type=F32
                )
            terms = gate[rows, :]
            value = jnp.concatenate(
                [
                    jnp.where(free_first, terms, value[:, 0:128]),
                    value[:, 128:last],
                    jnp.where(free_last, terms, value[:, last:lanes]),
                ],
                axis=1,
            )
            for at in range(size // cap):
                s = c * (size // cap) + at
                fbuf[z, s] = fold(value[at * cap : (at + 1) * cap])

                @pl.when(jnp.logical_not(is_here(z, s)))
                def _():
                    to_group(z, s, zp, my_group).start()

                @pl.when(is_here(z, s))
                def _():
                    vbuf[z, s] = fbuf[z, s]

    for z in range(2):
        for s in range(groups):

            @pl.when(jnp.logical_not(is_here(z, s)))
            def _():
                arriving = to_group(z, s, z, s)
                arriving.wait_recv()
                arriving.wait_send()

    count = experts * 16
    placed = pbuf[...].reshape(count, slots)
    scaled = wbuf[...].reshape(count, slots)
    row_group = lax.div(lax.broadcasted_iota(jnp.int32, (slots, 128), 0), cap)
    lane_group = lax.broadcasted_iota(jnp.int32, (slots, 128), 1)
    summed, terms = None, None
    for z in range(2):
        whole = jnp.concatenate([unfold(vbuf[z, g]) for g in range(groups)], axis=0)
        arrived = whole.astype(BF16)
        spread = jnp.where(
            row_group == lane_group,
            free_lanes(whole[:, 0:128], whole[:, last:lanes]), 0.0,
        ).astype(BF16)
        more = lax.dot_general(scaled, arrived, NN, preferred_element_type=F32)
        more_terms = lax.dot_general(placed, spread, NN, preferred_element_type=F32)
        summed = more if summed is None else summed + more
        terms = more_terms if terms is None else terms + more_terms
    tokens_in = xbuf[...].reshape(count, lanes)
    key = keys(free_lanes(tokens_in[:, 0:128], tokens_in[:, last:lanes]))
    of_group = jnp.floor((key + 0.5) * (1.0 / cap))
    routed = jnp.zeros(key.shape, F32)
    for g in range(groups):
        routed = jnp.where(of_group == g, terms[:, g : g + 1], routed)
    lane_all = lax.broadcasted_iota(jnp.int32, key.shape, 1)
    ubuf[:, :, 0:128] = jnp.where(lane_all < 64 * odd, routed, summed[:, 0:128]).reshape(
        experts, 16, 128
    )
    ubuf[:, :, 128:last] = summed[:, 128:last].reshape(experts, 16, last - 128)
    ubuf[:, :, last:lanes] = jnp.where(
        lane_all >= 64 + 64 * odd, pltpu.roll(routed, 64, 1), summed[:, last:lanes]
    ).reshape(experts, 16, 128)

    ubf[...] = ubuf[...].astype(BF16)
    nearer = {}
    for of in (-6, 6, -3, 3, 0):
        for route in routes[of]:
            at = aside.index(route)
            nearer[route] = send(
                ubf.at[block(of - route[0])], gn_in.at[at], gn_sem, at, in_ring(-route[0])
            )

    def with_aside(of):
        value = ubuf[block(of)]
        for route in routes[of]:
            nearer[route].wait_recv()
            value = value + gn_in[aside.index(route)].astype(F32)
        return value

    def go_back(value, index, target):
        gr_out[index] = value.astype(BF16)
        return send(gr_out.at[index], gr_in.at[index], gr_sem, index, target)

    right_2 = go_back(with_aside(6), 3, right)
    left_2 = go_back(with_aside(-6), 2, left)
    value = with_aside(3)
    right_2.wait_recv()
    right_1 = go_back(value + gr_in[3].astype(F32), 1, right)
    value = with_aside(-3)
    left_2.wait_recv()
    left_1 = go_back(value + gr_in[2].astype(F32), 0, left)
    value = with_aside(0)
    right_1.wait_recv()
    left_1.wait_recv()
    value = value + gr_in[0].astype(F32) + gr_in[1].astype(F32)

    block_rows[...] = value
    for b in range(SPLIT):
        fin[b] = block_rows[2 * b : 2 * b + 2, :]
    hbuf[q] = fin[q]
    copies = []
    for d in range(1, SPLIT):
        target = lax.rem(q + d, SPLIT)
        copies.append(send(fin.at[target], hbuf.at[q], h_sem, d - 1, in_block(target)))
    for copy in copies:
        copy.wait_recv()
    for m in range(SPLIT // 2):
        even, uneven = hbuf[2 * m], hbuf[2 * m + 1]
        base = 2 * part * m
        out_ref[:, base : base + last] = even[:, 0:last].astype(BF16)
        out_ref[:, base + last : base + lanes] = jnp.where(
            lane2 < 64, even[:, last:lanes], uneven[:, 0:128]
        ).astype(BF16)
        out_ref[:, base + lanes : base + 2 * part] = uneven[:, 128:lanes].astype(BF16)
    routing = pltpu.roll(hbuf[0][:, last:lanes] + hbuf[2][:, last:lanes], 64, 1)
    routing = routing + hbuf[1][:, 0:128] + hbuf[3][:, 0:128]
    routing_ref[...] = routing[:, 0:8]
    for copy in started:
        copy.wait_send()


def on_device(out_grad, routing_weight, expert_ids, slot_index, w_gate, w_up, w_down, pre_act):
    groups = lax.axis_size("group")
    experts = lax.axis_size("inner") // SPLIT
    cap = pre_act.shape[1] // groups
    width = out_grad.shape[1]
    lanes = -(-(width // SPLIT) // 128) * 128
    slots = groups * cap
    hidden = w_down.shape[0]
    vmem = pltpu.VMEM
    dma = pltpu.SemaphoreType.DMA
    scratch = [
        vmem(out_grad.shape, BF16),
        vmem(routing_weight.shape, BF16),
        vmem(expert_ids.shape, jnp.int32),
        vmem(slot_index.shape, jnp.int32),
        vmem((4, 2, hidden, lanes), BF16),
        vmem((4, 2, lanes, 256), BF16),
        vmem((2, slots, hidden), BF16),
        vmem((SPLIT, 2, lanes), F32),
        vmem((SPLIT, 2, lanes), F32),
        vmem((16, lanes), F32),
        vmem((experts, 16, lanes), BF16),
        vmem((experts, 16, slots), BF16),
        vmem((experts, 16, slots), BF16),
        vmem((groups, 2 * cap, lanes // 2), BF16),
        vmem((2, groups, 2 * cap, lanes // 2), BF16),
        vmem((2, slots, lanes), BF16),
        vmem((4, slots, hidden), BF16),
        vmem((4, slots, hidden), BF16),
        vmem((slots, hidden), F32),
        vmem((4, slots, 256), BF16),
        vmem((slots, 128), F32),
        vmem((2, groups, 2 * cap, lanes // 2), BF16),
        vmem((2, groups, 2 * cap, lanes // 2), BF16),
        vmem((experts, 16, lanes), F32),
        vmem((experts, 16, lanes), BF16),
        vmem((4, 16, lanes), BF16),
        vmem((4, 16, lanes), BF16),
        vmem((11, 16, lanes), BF16),
        vmem((SPLIT, 2, lanes), F32),
        vmem((SPLIT, 2, lanes), F32),
        dma((11,)),
        dma((2, SPLIT)),
        dma((2, 4)),
        dma((2, 11)),
        dma((2, 6)),
        dma((2, 12)),
        dma((2, 2 * groups)),
        dma((2, 4 * CHUNKS)),
        dma((2, 4 * CHUNKS)),
        dma((2, 2 * groups)),
        dma((2, 4)),
        dma((2, 11)),
        dma((2, SPLIT)),
    ]
    in_vmem = pl.BlockSpec(memory_space=pltpu.VMEM)
    anywhere = pl.BlockSpec(memory_space=pl.ANY)
    return pl.pallas_call(
        functools.partial(kernel, groups, experts, cap),
        out_shape=(
            jax.ShapeDtypeStruct(out_grad.shape, BF16),
            jax.ShapeDtypeStruct(expert_ids.shape, F32),
        ),
        in_specs=[anywhere] * 8,
        out_specs=(in_vmem, in_vmem),
        scratch_shapes=scratch,
        compiler_params=pltpu.CompilerParams(
            collective_id=0, has_side_effects=True, vmem_limit_bytes=60 * 2**20
        ),
        name="routed_backward",
    )(out_grad, routing_weight, expert_ids, slot_index, w_gate, w_up, w_down, pre_act)


def solution(mesh):
    token = P(("group", "inner"), None)
    in_specs = (
        token, token, token, token,
        P(None, ("group", "inner")),
        P(None, ("group", "inner")),
        P(("group", "inner"), None),
        P(None, None, ("group", "inner")),
    )
    return jax.shard_map(
        on_device, mesh=mesh, in_specs=in_specs, out_specs=(token, token), check_vma=False
    )
```
